32 devices in a mesh: dp: 4 (over x, core), expert: 8 (over z, y).
Axes of the slice: x: 2, y: 2, z: 4, core: 2. Of those that a mesh axis runs over, the one named last changes fastest.
Arguments:
- tokens: bfloat16 [512, 4096], P(('dp', 'expert')), may hold values from -6 to 6
- routes: int32 [512, 8], P(('dp', 'expert')), may hold values from 0 to 15, all different within a row; in each aligned block of 16 rows (0 to 15, 16 to 31, ...) at most 16 rows name the same one
- route_gates: float32 [512, 8], P(('dp', 'expert')), may hold values from 0.02 to 0.5
- placement: int32 [16], replicated, may hold values from 0 to 15, each once
- swap_flags: int32 [16], replicated, may hold values from 0 to 1, as said below
- gate_weight: bfloat16 [8, 4096, 1536], P('expert', None, 'dp'), may hold values from -0.09375 to 0.09375
- up_weight: bfloat16 [8, 4096, 1536], P('expert', None, 'dp'), may hold values from -0.09375 to 0.09375
- down_weight: bfloat16 [8, 1536, 4096], P('expert', 'dp'), may hold values from -0.21875 to 0.21875
Outputs:
- layer_out: bfloat16 [512, 4096], P(('dp', 'expert'))
The draws below stay inside these ranges and needn't reach their ends.
Inputs may be any that keep to these rules, and one draw needn't show every extreme that they name: `routes`: each row names 8 different experts; among the 16 rows of one device no expert is named more than 16 times, a bound that some block reaches. `placement`: A permutation of the 16 positions. swap_flags[P] equals swap_flags[(P + 8) mod 16].
All inputs are finite; a program needn't handle non-finite values.
Results may differ from the reference program's by a relative error of at most 0.0065.
Values may be sent and summed in bfloat16 or wider, within the bound.
No kernel may reach another device: no remote copies, remote signals or barrier semaphores. Data moves between devices by JAX's collectives and lax.ppermute only.
A program may use at most 128 MiB of HBM per device.

```python
import math
import jax
import jax.numpy as jnp
import numpy as np
from jax import lax

D = 4096
FF = 768
TOP = 8
TOK_DEV = 16
SLOTS = 2
EXPERTS = 16
MOST = 16
TOKENS = 512
N_DP = 4
N_EXPERT = 8


def draw_swap_flags(key, part):
    pair_bits = jax.random.randint(key, (EXPERTS // 2,), 0, 2, dtype=jnp.int32)
    return jnp.concatenate([pair_bits, pair_bits])


def levels(stream_key, shape, split, low, top_value):
    def one(dim, parts):
        heights = jax.random.uniform(jax.random.fold_in(jax.random.fold_in(stream_key, 6), dim), (parts,), jnp.float32, low / len(split), top_value / len(split))
        return jnp.repeat(jnp.exp(heights), shape[dim] // parts).reshape((-1,) + (1,) * (len(shape) - dim - 1))

    factor_of = one(*split[0])
    for cut in split[1:]:
        factor_of = factor_of * one(*cut)
    return factor_of


def assign_block(own_key, own, number, rows, amount, top, limit, slope):
    order = jax.random.permutation(own_key, amount)
    crowded, common = shares(amount, rows * top, limit, slope, True), shares(amount, rows * top, limit, slope, False)
    places = jnp.arange(amount)

    def named(tallies, turn):
        used = int((tallies > 0).sum())
        fixed = max(1, used // 4)
        moved = fixed + (places - fixed + turn * (used - fixed)) % max(1, amount - fixed)
        return jnp.zeros((amount,), jnp.int32).at[order[jnp.where(places < fixed, places, moved)]].set(jnp.asarray(tallies, jnp.int32))

    tallies = jnp.where(number % 4 == 0, named(crowded, number // 4), named(common, number - number // 4 - 1))
    mixed = jax.random.permutation(jax.random.fold_in(own, 3), amount)
    donor, sink = mixed[0:amount // 2 * 2:2], mixed[1:amount // 2 * 2:2]
    slack = jnp.minimum(tallies[donor] - 1, limit - tallies[sink]) // 2
    slack = jnp.where((donor == order[0]) | (sink == order[0]) | (tallies[sink] == 0), 0, jnp.maximum(slack, 0))
    moved = jax.random.randint(jax.random.fold_in(own, 4), (amount // 2,), 0, 1 << 20) % (slack + 1)
    tallies = tallies.at[donor].add(-moved).at[sink].add(moved)
    labels = jnp.searchsorted(jnp.cumsum(tallies), jnp.arange(rows * top), side="right").astype(jnp.int32)
    grid = labels.reshape(top, rows).T
    grid = grid[jax.random.permutation(jax.random.fold_in(own, 1), rows)]
    turn = jax.random.randint(jax.random.fold_in(own, 2), (rows, 1), 0, top)
    return jnp.take_along_axis(grid, (jnp.arange(top)[None, :] + turn) % top, axis=1)


def shares(amount, total, limit, skew, full):
    loads = [(1 << 20) // math.isqrt(rank ** skew) + 1 for rank in range(1, amount + 1)]
    largest = limit if full else min(limit, max(-(-total // amount), total * loads[0] // sum(loads)))
    least = 1 if total - largest >= amount - 1 else 0
    counts, spare = [largest] + [least] * (amount - 1), total - largest - least * (amount - 1)
    while spare > 0:
        candidates = [i for i in range(1, amount) if counts[i] < largest] or [i for i in range(1, amount) if counts[i] < limit]
        mass, budget = sum([loads[i] for i in candidates]), spare
        for i in candidates:
            addition = min(limit - counts[i], max(1, budget * loads[i] // mass), spare)
            counts[i] = counts[i] + addition
            spare = spare - addition
    return np.array(counts)


def normal_values(own_key, dims, scale, reach, split=(), kind=jnp.bfloat16):
    level = levels(own_key, dims, split, -0.22, 0.18) if split else 1.0
    result = jax.random.normal(own_key, dims, jnp.float32) * scale * level
    return jnp.minimum(jnp.maximum(result, -reach), reach).astype(kind)


def setup_inputs(seed: int = 0) -> dict:
    arg_keys = jax.random.split(jax.random.key(seed), 9)
    tokens = normal_values(arg_keys[0], (TOKENS, D), 1.0, 6.0, ((0, 32),))
    routes_keys = jax.random.split(jax.random.fold_in(arg_keys[1], 1), TOKENS // TOK_DEV)
    routes_turns = jax.random.permutation(jax.random.fold_in(arg_keys[1], 3), TOKENS // TOK_DEV)
    routes = jax.vmap(lambda own, number: assign_block(jax.random.fold_in(arg_keys[1], 2), own, number, TOK_DEV, EXPERTS, TOP, MOST, 3))(routes_keys, routes_turns).reshape((TOKENS, TOP))
    route_gates = jnp.clip(jnp.exp(math.log(0.5) - 3.218876 * jax.random.uniform(arg_keys[2], (TOKENS, TOP), jnp.float32) ** levels(arg_keys[2], (TOKENS, TOP), ((0, 32),), -0.2, 0.2)), 0.02, 0.5)
    placement = jax.random.permutation(arg_keys[3], EXPERTS).astype(jnp.int32)
    swap_flags = draw_swap_flags(jax.random.fold_in(arg_keys[8], 71), 0)
    gate_weight = normal_values(arg_keys[5], (N_EXPERT, D, SLOTS * FF), D ** -0.5, 0.09375, ((0, 8), (2, 4)))
    up_weight = normal_values(arg_keys[6], (N_EXPERT, D, SLOTS * FF), D ** -0.5, 0.09375, ((0, 8), (2, 4)))
    down_weight = normal_values(arg_keys[7], (N_EXPERT, SLOTS * FF, D), FF ** -0.5, 0.21875, ((0, 8), (1, 4)))
    return dict(tokens=tokens, routes=routes, route_gates=route_gates, placement=placement, swap_flags=swap_flags, gate_weight=gate_weight, up_weight=up_weight, down_weight=down_weight)


def reference(tokens, routes, route_gates, placement, swap_flags, gate_weight, up_weight, down_weight):
    experts = placement.shape[0]
    slot_count = experts // N_EXPERT
    half_width = FF // 2
    capacity = N_DP * N_EXPERT * MOST
    flags_at = swap_flags[placement]
    holder = jnp.where(flags_at == 1, (placement + experts // 2) % experts, placement).astype(jnp.int32)

    def per_expert(accum_out, expert_id):
        matches = routes == expert_id
        gate_row = jnp.sum(jnp.where(matches, route_gates, jnp.float32(0.0)), axis=1)
        chosen = jnp.any(matches, axis=1)
        picked_rows = jnp.nonzero(chosen, size=capacity, fill_value=0)[0].astype(jnp.int32)
        valid = (jnp.arange(capacity, dtype=jnp.int32) < jnp.sum(chosen.astype(jnp.int32))).astype(jnp.float32)
        received = tokens[picked_rows].astype(jnp.float32)
        position = holder[expert_id]
        column = (position // slot_count).astype(jnp.int32)
        slot_id = (position % slot_count).astype(jnp.int32)
        start = (slot_id * FF).astype(jnp.int32)
        zero = jnp.int32(0)
        block_gate = lax.dynamic_slice(gate_weight, (column, zero, start), (1, D, FF))[0]
        block_up = lax.dynamic_slice(up_weight, (column, zero, start), (1, D, FF))[0]
        block_down = lax.dynamic_slice(down_weight, (column, start, zero), (1, FF, D))[0]
        expert_sum = jnp.zeros((capacity, D), jnp.float32)
        for half_id in range(2):
            lower = half_id * half_width
            upper = lower + half_width
            gate_act = jnp.dot(received, block_gate[:, lower:upper].astype(jnp.float32), precision=lax.Precision.HIGHEST)
            up_act = jnp.dot(received, block_up[:, lower:upper].astype(jnp.float32), precision=lax.Precision.HIGHEST)
            hidden = (jax.nn.silu(gate_act) * up_act).astype(jnp.bfloat16)
            hidden = lax.optimization_barrier(hidden).astype(jnp.float32)
            partial_value = jnp.dot(hidden, block_down[lower:upper, :].astype(jnp.float32), precision=lax.Precision.HIGHEST).astype(jnp.bfloat16)
            partial_value = lax.optimization_barrier(partial_value).astype(jnp.float32)
            expert_sum = expert_sum + partial_value
        expert_rows = lax.optimization_barrier(expert_sum.astype(jnp.bfloat16)).astype(jnp.float32)
        scale = gate_row[picked_rows] * valid
        accum_out = accum_out.at[picked_rows].add(expert_rows * scale[:, None])
        return accum_out, None

    start_out = jnp.zeros((TOKENS, D), jnp.float32)
    final_out, unused = lax.scan(per_expert, start_out, jnp.arange(experts, dtype=jnp.int32))
    return final_out.astype(jnp.bfloat16)
```

```python
import jax
import jax.numpy as jnp
from jax import lax
from jax.sharding import PartitionSpec as P

MESH_AXES = ("dp", "expert")
F32 = jnp.float32
BF16 = jnp.bfloat16


def expert_block(received, w_gate, w_up, w_down):
    gate_act = jnp.dot(received, w_gate, preferred_element_type=F32)
    up_act = jnp.dot(received, w_up, preferred_element_type=F32)
    hidden = (jax.nn.silu(gate_act) * up_act).astype(BF16)
    return jnp.dot(hidden, w_down, preferred_element_type=F32)


def holder_of(placement, swap_flags):
    experts = placement.shape[0]
    ids = jnp.arange(experts, dtype=jnp.int32)
    flag_at = jnp.sum(jnp.where(placement[:, None] == ids[None, :], swap_flags[None, :], 0), axis=1)
    return jnp.where(flag_at == 0, placement, (placement + experts // 2) % experts)


def routed_position(routes, holder):
    ids = jnp.arange(holder.shape[0], dtype=jnp.int32)
    return jnp.sum(jnp.where(routes[..., None] == ids, holder, 0), axis=-1)


NX, NC, NZ, NY = 2, 2, 4, 2


def flat(x, c, z, y):
    return (x * NC + c) * (NZ * NY) + z * NY + y


def moved(value, to):
    pairs = [
        (flat(x, c, z, y), flat(*to(x, c, z, y)))
        for x in range(NX)
        for c in range(NC)
        for z in range(NZ)
        for y in range(NY)
    ]
    return lax.ppermute(value, MESH_AXES, pairs)


def over_x(value):
    return moved(value, lambda x, c, z, y: (1 - x, c, z, y))


def over_y(value):
    return moved(value, lambda x, c, z, y: (x, c, z, 1 - y))


def over_core(value):
    return moved(value, lambda x, c, z, y: (x, 1 - c, z, y))


def along_z(value, by):
    return moved(value, lambda x, c, z, y: (x, c, (z + by) % NZ, y))


def plane_gather(block):
    half = block.shape[0] // 2
    from_x = over_x(block)
    from_y = over_y(block)
    first = over_y(from_x[:half])
    second = over_x(from_y[half:])
    return jnp.concatenate([block, from_x, from_y, first, second], axis=0)


def plane_sum(rows):
    size = rows.shape[0] // 4
    half = size // 2
    wide = rows.astype(F32)
    mine, for_x, for_y, for_diag = (wide[i * size : (i + 1) * size] for i in range(4))
    diag = rows[3 * size :]
    add_x = over_y(diag[:half]).astype(F32)
    add_y = over_x(diag[half:]).astype(F32)
    for_x = jnp.concatenate([for_x[:half] + add_x, for_x[half:]], axis=0).astype(BF16)
    for_y = jnp.concatenate([for_y[:half], for_y[half:] + add_y], axis=0).astype(BF16)
    return mine + over_x(for_x).astype(F32) + over_y(for_y).astype(F32)


def on_device_plane(
    tokens, routes, route_gates, placement, swap_flags, gate_weight, up_weight, down_weight
):
    rows = tokens.shape[0]
    w_gate, w_up, w_down = gate_weight[0], up_weight[0], down_weight[0]
    dp_at, expert_at = lax.axis_index("dp"), lax.axis_index("expert")
    x_at, c_at, z_at, y_at = dp_at // NC, dp_at % NC, expert_at // NY, expert_at % NY
    position = expert_at * NX + x_at

    all_routes = lax.all_gather(routes, MESH_AXES, axis=0)
    all_gates = lax.all_gather(route_gates, MESH_AXES, axis=0)
    target = routed_position(all_routes, holder_of(placement, swap_flags))
    row_gate = jnp.sum(jnp.where(target == position, all_gates, 0.0), axis=-1)
    row_gate = row_gate.reshape(NX, NC, NZ, NY, rows)

    def gates_from(c, shifts):
        def at(dx, dy):
            return jnp.concatenate(
                [row_gate[x_at ^ dx, c, (z_at - k) % NZ, y_at ^ dy] for k in shifts], axis=0
            )

        return jnp.concatenate([at(0, 0), at(1, 0), at(0, 1), at(1, 1)], axis=0)

    from_z = {k: along_z(tokens, k) for k in (1, 3, 2)}
    shift_sets = ((0,), (1, 3, 2))
    starts = (tokens, jnp.concatenate([from_z[k] for k in shift_sets[1]], axis=0))
    sums = []
    for shifts, start in zip(shift_sets, starts):
        own_rows = plane_gather(start)
        other_rows = over_core(own_rows)
        own = expert_block(own_rows, w_gate, w_up, w_down)
        other = expert_block(other_rows, w_gate, w_up, w_down)
        own = own * gates_from(c_at, shifts)[:, None]
        other = (other * gates_from(1 - c_at, shifts)[:, None]).astype(BF16)
        both = (own + over_core(other).astype(F32)).astype(BF16)
        sums.append(plane_sum(both))
    total = sums[0]
    for i, k in enumerate(shift_sets[1]):
        part = sums[1][i * rows : (i + 1) * rows].astype(BF16)
        total = total + along_z(part, NZ - k).astype(F32)
    return total.astype(BF16)


def on_device_lanes(
    tokens, routes, route_gates, placement, swap_flags, gate_weight, up_weight, down_weight
):
    tok_dev, features = tokens.shape
    route_count = routes.shape[1]
    columns = lax.axis_size("expert")
    replicas = lax.axis_size("dp")
    slot_count = replicas // 2
    experts = slot_count * columns
    capacity = 2 * tok_dev * route_count // experts
    lane_count = experts * capacity
    expert_ids = jnp.arange(experts, dtype=jnp.int32)
    flat_routes = routes.reshape(-1)
    matches = (flat_routes[:, None] == expert_ids[None, :]).astype(jnp.int32)
    target = routed_position(flat_routes, holder_of(placement, swap_flags))
    ranking = jnp.sum(matches * (jnp.cumsum(matches, axis=0) - 1), axis=1)
    column = target // slot_count
    slot_id = target % slot_count
    lane_index = (slot_id * columns + column) * capacity + ranking
    pair_row = jnp.arange(tok_dev * route_count, dtype=jnp.int32) // route_count
    lane_hit = (jnp.arange(lane_count, dtype=jnp.int32)[:, None] == lane_index[None, :]).astype(F32)
    row_hit = (jnp.arange(tok_dev, dtype=jnp.int32)[:, None] == pair_row[None, :]).astype(F32)
    selector = jnp.dot(lane_hit, row_hit.T, precision=lax.Precision.HIGHEST).astype(BF16)
    combine = jnp.dot(
        row_hit * route_gates.reshape(-1)[None, :], lane_hit.T, precision=lax.Precision.HIGHEST
    )
    outgoing = jnp.dot(selector, tokens, preferred_element_type=F32).astype(BF16)
    outgoing = outgoing.reshape(slot_count, columns, capacity, features)

    def exchanged(value):
        value = lax.all_to_all(value, "dp", split_axis=0, concat_axis=0, tiled=True)
        return lax.all_to_all(value, "expert", split_axis=1, concat_axis=1, tiled=True)

    arrived = exchanged(jnp.repeat(outgoing, 2, axis=0))
    partial_value = expert_block(
        arrived.reshape(-1, features), gate_weight[0], up_weight[0], down_weight[0]
    ).astype(BF16)
    returned = exchanged(partial_value.reshape(replicas, columns, capacity, features))
    halves = returned.reshape(slot_count, 2, columns, capacity, features)
    summed = (halves[:, 0].astype(F32) + halves[:, 1].astype(F32)).astype(BF16)
    expert_rows = summed.reshape(lane_count, features)
    layer_out = jnp.dot(combine, expert_rows.astype(F32), precision=lax.Precision.HIGHEST)
    return layer_out.astype(BF16)


def solution(mesh):
    planes = mesh.shape["dp"] == NX * NC and mesh.shape["expert"] == NZ * NY
    return jax.shard_map(
        on_device_plane if planes else on_device_lanes,
        mesh=mesh,
        in_specs=(
            P(MESH_AXES, None),
            P(MESH_AXES, None),
            P(MESH_AXES, None),
            P(),
            P(),
            P("expert", None, "dp"),
            P("expert", None, "dp"),
            P("expert", "dp", None),
        ),
        out_specs=P(MESH_AXES, None),
        check_vma=False,
    )
```

```python
import functools

import jax
import jax.numpy as jnp
from jax import lax
from jax.experimental import pallas as pl
from jax.experimental.pallas import tpu as pltpu
from jax.sharding import PartitionSpec as P

MESH_AXES = ("dp", "expert")
F32 = jnp.float32
BF16 = jnp.bfloat16


def expert_block(received, w_gate, w_up, w_down):
    gate_act = jnp.dot(received, w_gate, preferred_element_type=F32)
    up_act = jnp.dot(received, w_up, preferred_element_type=F32)
    hidden = (jax.nn.silu(gate_act) * up_act).astype(BF16)
    return jnp.dot(hidden, w_down, preferred_element_type=F32)


def holder_of(placement, swap_flags):
    experts = placement.shape[0]
    ids = jnp.arange(experts, dtype=jnp.int32)
    flag_at = jnp.sum(jnp.where(placement[:, None] == ids[None, :], swap_flags[None, :], 0), axis=1)
    return jnp.where(flag_at == 0, placement, (placement + experts // 2) % experts)


def routed_position(routes, holder):
    ids = jnp.arange(holder.shape[0], dtype=jnp.int32)
    return jnp.sum(jnp.where(routes[..., None] == ids, holder, 0), axis=-1)


NX, NC, NZ, NY = 2, 2, 4, 2
TAIL = 128
PARTS = 3
ORDER = (0, 1, 3, 2)
COST = 20

IN_VMEM = pl.BlockSpec(memory_space=pltpu.VMEM)
IN_SMEM = pl.BlockSpec(memory_space=pltpu.SMEM)
IN_HBM = pl.BlockSpec(memory_space=pltpu.HBM)


def flat(x, c, z, y):
    return (x * NC + c) * (NZ * NY) + z * NY + y


def moved(value, to):
    pairs = [
        (flat(x, c, z, y), flat(*to(x, c, z, y)))
        for x in range(NX)
        for c in range(NC)
        for z in range(NZ)
        for y in range(NY)
    ]
    return lax.ppermute(value, MESH_AXES, pairs)


def over_first(value):
    return moved(value, lambda x, c, z, y: (x ^ 1 ^ c, c, z, y ^ c))


def over_second(value):
    return moved(value, lambda x, c, z, y: (x ^ c, c, z, y ^ 1 ^ c))


def over_core(value):
    return moved(value, lambda x, c, z, y: (x, 1 - c, z, y))


def along_z(value, by):
    return moved(value, lambda x, c, z, y: (x, c, z ^ by, y))


def kernel(body, name, outs, arrays, scalars=(), scratch=(), far=0, vmem=2, flops=0):
    placed = [pltpu.with_memory_space_constraint(a, pltpu.HBM) for a in arrays[:far]]
    placed += [pltpu.with_memory_space_constraint(a, pltpu.VMEM) for a in arrays[far:]]
    return pl.pallas_call(
        body,
        name=name,
        out_shape=[pltpu.VMEM(shape, dtype) for shape, dtype in outs],
        in_specs=[IN_SMEM] * len(scalars) + [IN_HBM] * far + [IN_VMEM] * (len(arrays) - far),
        out_specs=[IN_VMEM] * len(outs),
        scratch_shapes=list(scratch),
        compiler_params=pltpu.CompilerParams(vmem_limit_bytes=vmem * 2**20),
        cost_estimate=pl.CostEstimate(flops=flops, bytes_accessed=0, transcendentals=0),
    )(*scalars, *placed)


def label_body(
    tokens, routes, gates, placement, flags, out, token_at, route_at, gate_at, place_at, flag_at, sems
):
    rows, features = tokens.shape
    experts = placement.shape[0]
    pairs = (
        (placement, place_at),
        (flags, flag_at),
        (routes, route_at),
        (gates, gate_at),
        (tokens, token_at),
    )
    copies = [pltpu.make_async_copy(a, b, sems.at[i]) for i, (a, b) in enumerate(pairs)]
    for copy in copies:
        copy.start()
    for copy in copies:
        copy.wait()
    out[:, :features] = token_at[...]
    named = route_at[...].T
    row_gates = gate_at[...].T
    target = jnp.zeros_like(named)
    for x in range(experts):
        held = place_at[x]
        held = jnp.where(flag_at[held] == 0, held, (held + experts // 2) % experts)
        target = jnp.where(named == x, held, target)
    lane = lax.broadcasted_iota(jnp.int32, (rows, TAIL), 1)
    weight = jnp.zeros((rows, TAIL), F32)
    for k in range(named.shape[1]):
        weight += jnp.where(lane % experts == target[:, k : k + 1], row_gates[:, k : k + 1], 0.0)
    high = weight.astype(BF16)
    rest = weight - high.astype(F32)
    middle = rest.astype(BF16)
    low = (rest - middle.astype(F32)).astype(BF16)
    tail = jnp.where(lane < experts, high.astype(F32), 0.0)
    tail = jnp.where((lane >= experts) & (lane < 2 * experts), middle.astype(F32), tail)
    tail = jnp.where((lane >= 2 * experts) & (lane < PARTS * experts), low.astype(F32), tail)
    out[:, features:] = tail.astype(BF16)


def labelled(tokens, routes, route_gates, placement, swap_flags):
    rows, features = tokens.shape
    arrays = (tokens, routes.T, route_gates.T, placement, swap_flags)
    outs = [((rows, features + TAIL), BF16)]
    scratch = [pltpu.VMEM(a.shape, a.dtype) for a in arrays[:3]]
    scratch += [pltpu.SMEM(a.shape, a.dtype) for a in arrays[3:]]
    scratch.append(pltpu.SemaphoreType.DMA((len(arrays),)))
    [out] = kernel(label_body, "label", outs, arrays, scratch=scratch, far=len(arrays))
    return out


def stage_body(*refs):
    *pairs, sems = refs
    count = len(pairs) // 2
    copies = [pltpu.make_async_copy(pairs[i], pairs[count + i], sems.at[i]) for i in range(count)]
    for copy in copies:
        copy.start()
    for copy in copies:
        copy.wait()


def staged(weights):
    outs = [(w.shape, w.dtype) for w in weights]
    scratch = [pltpu.SemaphoreType.DMA((len(weights),))]
    return kernel(stage_body, "stage", outs, weights, scratch=scratch, far=len(weights))


def pack_body(groups, *refs):
    blocks, outs = list(refs[: sum(groups)]), refs[len(refs) - len(groups) :]
    for out, count in zip(outs, groups):
        at = 0
        for _ in range(count):
            block = blocks.pop(0)
            out[at : at + block.shape[0], :] = block[...]
            at += block.shape[0]


def packed(*groups, after=()):
    outs = [((sum(b.shape[0] for b in g), g[0].shape[1]), g[0].dtype) for g in groups]
    body = functools.partial(pack_body, tuple(len(g) for g in groups))
    return kernel(body, "pack", outs, [b for g in groups for b in g] + list(after))


def expert_body(features, experts, mine, others, w_gate, w_up, w_down, *refs):
    kept, sent, partner, joined, hidden = refs
    count, half = mine.shape[0], kept.shape[0]
    position = lax.axis_index("expert") * NX + lax.div(lax.axis_index("dp"), NC)
    joined[:count, :] = mine[...]
    joined[count:, :] = others[...]
    x = joined[:, :features]
    gate_act = jnp.dot(x, w_gate[...], preferred_element_type=F32)
    up_act = jnp.dot(x, w_up[...], preferred_element_type=F32)
    hidden[...] = (gate_act / (1.0 + jnp.exp(-gate_act)) * up_act).astype(BF16)
    tail = joined[:, features:].astype(F32)
    lane = lax.broadcasted_iota(jnp.int32, tail.shape, 1)
    here = (lane % experts == position) & (lane < PARTS * experts)
    row_gate = jnp.sum(jnp.where(here, tail, 0.0), axis=1, keepdims=True)
    h = hidden[...]
    step = 512
    for c in range(0, features, step):
        columns = slice(c, c + step)
        value = jnp.dot(h, w_down[:, columns], preferred_element_type=F32) * row_gate
        value = value.astype(BF16)
        kept[:, columns] = value[:half]
        sent[:, columns] = value[half:count]
        partner[:, columns] = value[count:]


def expert_rows(mine, others, weights, experts):
    count, width = mine.shape
    features, hidden_units = weights[0].shape
    return kernel(
        functools.partial(expert_body, features, experts),
        "expert",
        [((n, features), BF16) for n in (count // 2, count // 2, count)],
        (mine, others, *weights),
        scratch=[pltpu.VMEM((2 * count, width), BF16), pltpu.VMEM((2 * count, hidden_units), BF16)],
        vmem=6,
        flops=COST * 12 * count * features * hidden_units,
    )


def core_sum_body(sent, received, out):
    rows = received[sent.shape[0] :, :].astype(F32)
    out[...] = (sent[...].astype(F32) + rows).astype(BF16)


def part_sum_body(kept, from_core, received, mine, passed):
    rows = mine.shape[0]

    def total(at):
        return (kept[at, :].astype(F32) + from_core[at, :].astype(F32)) + received[at, :].astype(F32)

    mine[...] = total(slice(0, rows))
    passed[...] = total(slice(rows, 2 * rows)).astype(BF16)


def plane_sum_body(mine, received, out):
    out[...] = (mine[...] + received[...].astype(F32)).astype(out.dtype)


def final_sum_body(*refs):
    *parts, out = refs
    total = parts[0][...].astype(F32)
    for part in parts[1:]:
        total += part[...].astype(F32)
    out[...] = total.astype(BF16)


def on_device_plane(
    tokens, routes, route_gates, placement, swap_flags, gate_weight, up_weight, down_weight
):
    rows, features = tokens.shape
    experts = placement.shape[0]
    weights = gate_weight[0], up_weight[0], down_weight[0]
    own = labelled(tokens, routes, route_gates, placement, swap_flags)
    weights = staged(weights)
    from_z = {k: along_z(own, k) for k in (3, 1, 2)}
    near = {0: over_first(own)}
    pair0, block1, block3 = packed([own, near[0]], [from_z[1]], [from_z[3]], after=weights[:1])
    blocks = {1: block1, 3: block3, 2: from_z[2]}
    pairs = {0: pair0}
    mine, others = {}, {}
    for step in ORDER:
        if step:
            [pairs[step]] = packed([blocks[step], over_first(blocks[step])])
        [mine[step]] = packed([pairs[step], over_second(pairs[step])])
        others[step] = over_core(mine[step])
    parts = []
    for step in ORDER:
        kept, sent, partner = expert_rows(mine[step], others[step], weights, experts)
        from_core = over_core(partner)
        [sent] = kernel(core_sum_body, "core_sum", [(sent.shape, BF16)], (sent, from_core))
        outs = [((rows, features), F32), ((rows, features), BF16)]
        arrays = (kept, from_core, over_second(sent))
        kept, sent = kernel(part_sum_body, "part_sum", outs, arrays)
        outs = [((rows, features), BF16 if step else F32)]
        [total] = kernel(plane_sum_body, "plane_sum", outs, (kept, over_first(sent)))
        parts.append(along_z(total, step) if step else total)
    [out] = kernel(final_sum_body, "final_sum", [((rows, features), BF16)], parts)
    return out


def on_device_lanes(
    tokens, routes, route_gates, placement, swap_flags, gate_weight, up_weight, down_weight
):
    tok_dev, features = tokens.shape
    route_count = routes.shape[1]
    columns = lax.axis_size("expert")
    replicas = lax.axis_size("dp")
    slot_count = replicas // 2
    experts = slot_count * columns
    capacity = 2 * tok_dev * route_count // experts
    lane_count = experts * capacity
    expert_ids = jnp.arange(experts, dtype=jnp.int32)
    flat_routes = routes.reshape(-1)
    matches = (flat_routes[:, None] == expert_ids[None, :]).astype(jnp.int32)
    target = routed_position(flat_routes, holder_of(placement, swap_flags))
    ranking = jnp.sum(matches * (jnp.cumsum(matches, axis=0) - 1), axis=1)
    column = target // slot_count
    slot_id = target % slot_count
    lane_index = (slot_id * columns + column) * capacity + ranking
    pair_row = jnp.arange(tok_dev * route_count, dtype=jnp.int32) // route_count
    lane_hit = (jnp.arange(lane_count, dtype=jnp.int32)[:, None] == lane_index[None, :]).astype(F32)
    row_hit = (jnp.arange(tok_dev, dtype=jnp.int32)[:, None] == pair_row[None, :]).astype(F32)
    selector = jnp.dot(lane_hit, row_hit.T, precision=lax.Precision.HIGHEST).astype(BF16)
    combine = jnp.dot(
        row_hit * route_gates.reshape(-1)[None, :], lane_hit.T, precision=lax.Precision.HIGHEST
    )
    outgoing = jnp.dot(selector, tokens, preferred_element_type=F32).astype(BF16)
    outgoing = outgoing.reshape(slot_count, columns, capacity, features)

    def exchanged(value):
        value = lax.all_to_all(value, "dp", split_axis=0, concat_axis=0, tiled=True)
        return lax.all_to_all(value, "expert", split_axis=1, concat_axis=1, tiled=True)

    arrived = exchanged(jnp.repeat(outgoing, 2, axis=0))
    partial_value = expert_block(
        arrived.reshape(-1, features), gate_weight[0], up_weight[0], down_weight[0]
    ).astype(BF16)
    returned = exchanged(partial_value.reshape(replicas, columns, capacity, features))
    halves = returned.reshape(slot_count, 2, columns, capacity, features)
    summed = (halves[:, 0].astype(F32) + halves[:, 1].astype(F32)).astype(BF16)
    expert_rows = summed.reshape(lane_count, features)
    layer_out = jnp.dot(combine, expert_rows.astype(F32), precision=lax.Precision.HIGHEST)
    return layer_out.astype(BF16)


def solution(mesh):
    planes = mesh.shape["dp"] == NX * NC and mesh.shape["expert"] == NZ * NY
    return jax.shard_map(
        on_device_plane if planes else on_device_lanes,
        mesh=mesh,
        in_specs=(
            P(MESH_AXES, None),
            P(MESH_AXES, None),
            P(MESH_AXES, None),
            P(),
            P(),
            P("expert", None, "dp"),
            P("expert", None, "dp"),
            P("expert", "dp", None),
        ),
        out_specs=P(MESH_AXES, None),
        check_vma=False,
    )
```

```python
import functools

import jax
import jax.numpy as jnp
from jax import lax
from jax.experimental import pallas as pl
from jax.experimental.pallas import tpu as pltpu
from jax.sharding import PartitionSpec as P

MESH_AXES = ("dp", "expert")
F32 = jnp.float32
BF16 = jnp.bfloat16


def expert_block(received, w_gate, w_up, w_down):
    gate_act = jnp.dot(received, w_gate, preferred_element_type=F32)
    up_act = jnp.dot(received, w_up, preferred_element_type=F32)
    hidden = (jax.nn.silu(gate_act) * up_act).astype(BF16)
    return jnp.dot(hidden, w_down, preferred_element_type=F32)


def holder_of(placement, swap_flags):
    experts = placement.shape[0]
    ids = jnp.arange(experts, dtype=jnp.int32)
    flag_at = jnp.sum(jnp.where(placement[:, None] == ids[None, :], swap_flags[None, :], 0), axis=1)
    return jnp.where(flag_at == 0, placement, (placement + experts // 2) % experts)


def routed_position(routes, holder):
    ids = jnp.arange(holder.shape[0], dtype=jnp.int32)
    return jnp.sum(jnp.where(routes[..., None] == ids, holder, 0), axis=-1)


NX, NC, NZ, NY = 2, 2, 4, 2
TAIL = 128
PARTS = 3
PIECES = 4
SEQUENCE = (
    "pair0",
    "block3 block1",
    "stage2",
    "block2",
    "pair3 mine0 pair1",
    "stage1",
    "stage0",
    "pair2",
    "mine3",
    "mine1",
    "expert0",
    "expert3",
    "expert1",
    "core0 core3 mine2",
    "expert2",
    "core1 far3",
    "far0",
    "core2",
    "near3 far2 far1",
    "near0",
    "near2 near1",
    "fold3",
    "fold2",
    "fold1",
)
WEIGHT = 3

IN_VMEM = pl.BlockSpec(memory_space=pltpu.VMEM)
IN_HBM = pl.BlockSpec(memory_space=pltpu.HBM)


def flat(x, c, z, y):
    return (x * NC + c) * (NZ * NY) + z * NY + y


def moved(value, to):
    pairs = [
        (flat(x, c, z, y), flat(*to(x, c, z, y)))
        for x in range(NX)
        for c in range(NC)
        for z in range(NZ)
        for y in range(NY)
    ]
    return lax.ppermute(value, MESH_AXES, pairs)


def over_first(value):
    return moved(value, lambda x, c, z, y: (x ^ 1 ^ c, c, z, y ^ c))


def over_second(value):
    return moved(value, lambda x, c, z, y: (x ^ c, c, z, y ^ 1 ^ c))


def over_core(value):
    return moved(value, lambda x, c, z, y: (x, 1 - c, z, y))


def along_z(value, by):
    return moved(value, lambda x, c, z, y: (x, c, z ^ by, y))


class Order:
    def __init__(self):
        self.mark = ()

    def __call__(self, body, name, outs, arrays, scratch=(), far=0, vmem=2, flops=0, last=False):
        near = [pltpu.with_memory_space_constraint(a, pltpu.VMEM) for a in (*arrays[far:], *self.mark)]
        placed = [pltpu.with_memory_space_constraint(a, pltpu.HBM) for a in arrays[:far]]
        given, skipped, made = len(arrays), len(self.mark), len(outs)
        marks = [] if last else [((8, 128), F32)]

        def marked(*refs):
            rest = refs[given + skipped :]
            for mark in rest[made : made + len(marks)]:
                mark[...] = jnp.zeros((8, 128), F32)
            body(*refs[:given], *rest[:made], *rest[made + len(marks) :])

        results = pl.pallas_call(
            marked,
            name=name,
            out_shape=[pltpu.VMEM(shape, dtype) for shape, dtype in (*outs, *marks)],
            in_specs=[IN_HBM] * far + [IN_VMEM] * len(near),
            out_specs=[IN_VMEM] * (made + len(marks)),
            scratch_shapes=list(scratch),
            compiler_params=pltpu.CompilerParams(vmem_limit_bytes=vmem * 2**20),
            cost_estimate=pl.CostEstimate(flops=flops, bytes_accessed=0, transcendentals=0),
        )(*placed, *near)
        self.mark = results[made:]
        return results[:made]


def together(order, parts, last):
    def body(*refs):
        taken = 0
        made = sum(len(arrays) for _, _, arrays in parts)
        for part, outs, arrays in parts:
            part(*refs[taken : taken + len(arrays)], *refs[made : made + len(outs)])
            taken += len(arrays)
            made += len(outs)

    all_outs = [out for _, outs, _ in parts for out in outs]
    all_arrays = [a for _, _, arrays in parts for a in arrays]
    results = order(body, "sums", all_outs, all_arrays, last=last)
    split = []
    for _, outs, _ in parts:
        split.append(results[: len(outs)])
        results = results[len(outs) :]
    return split


def label_body(
    tokens, routes, gates, placement, flags, out, token_at, route_at, gate_at, place_at, flag_at, sems
):
    rows, features = tokens.shape
    experts = placement.shape[0]
    pairs = (
        (placement, place_at),
        (flags, flag_at),
        (routes, route_at),
        (gates, gate_at),
        (tokens, token_at),
    )
    copies = [pltpu.make_async_copy(a, b, sems.at[i]) for i, (a, b) in enumerate(pairs)]
    for copy in copies:
        copy.start()
    for copy in copies:
        copy.wait()
    out[:, :features] = token_at[...]
    named = route_at[...].T
    row_gates = gate_at[...].T
    target = jnp.zeros_like(named)
    for x in range(experts):
        held = place_at[x]
        held = jnp.where(flag_at[held] == 0, held, (held + experts // 2) % experts)
        target = jnp.where(named == x, held, target)
    lane = lax.broadcasted_iota(jnp.int32, (rows, TAIL), 1)
    weight = jnp.zeros((rows, TAIL), F32)
    for k in range(named.shape[1]):
        weight += jnp.where(lane % experts == target[:, k : k + 1], row_gates[:, k : k + 1], 0.0)
    high = weight.astype(BF16)
    rest = weight - high.astype(F32)
    middle = rest.astype(BF16)
    low = (rest - middle.astype(F32)).astype(BF16)
    tail = jnp.where(lane < experts, high.astype(F32), 0.0)
    tail = jnp.where((lane >= experts) & (lane < 2 * experts), middle.astype(F32), tail)
    tail = jnp.where((lane >= 2 * experts) & (lane < PARTS * experts), low.astype(F32), tail)
    out[:, features:] = tail.astype(BF16)


def labelled(order, tokens, routes, route_gates, placement, swap_flags):
    rows, features = tokens.shape
    arrays = (tokens, routes.T, route_gates.T, placement, swap_flags)
    outs = [((rows, features + TAIL), BF16)]
    scratch = [pltpu.VMEM(a.shape, a.dtype) for a in arrays[:3]]
    scratch += [pltpu.SMEM(a.shape, a.dtype) for a in arrays[3:]]
    scratch.append(pltpu.SemaphoreType.DMA((len(arrays),)))
    [out] = order(label_body, "label", outs, arrays, scratch=scratch, far=len(arrays))
    return out


def stage_body(source, out, sems):
    size = source.shape[0] // PIECES
    pieces = [pl.ds(i * size, size) for i in range(PIECES)]
    copies = [
        pltpu.make_async_copy(source.at[piece], out.at[piece], sems.at[i])
        for i, piece in enumerate(pieces)
    ]
    for copy in copies:
        copy.start()
    for copy in copies:
        copy.wait()


def staged(order, weight):
    outs = [(weight.shape, weight.dtype)]
    scratch = [pltpu.SemaphoreType.DMA((PIECES,))]
    [result] = order(stage_body, "stage", outs, (weight,), scratch, far=1)
    return result


def pack_body(block, received, out):
    count = block.shape[0]
    out[:count, :] = block[...]
    out[count:, :] = received[...]


def block_body(received, out):
    out[...] = received[...]


def expert_body(features, experts, mine, others, w_gate, w_up, w_down, *refs):
    kept, sent, partner_kept, partner_sent, joined, hidden = refs
    count, half = mine.shape[0], kept.shape[0]
    position = lax.axis_index("expert") * NX + lax.div(lax.axis_index("dp"), NC)
    joined[:count, :] = mine[...]
    joined[count:, :] = others[...]
    x = joined[:, :features]
    gate_act = jnp.dot(x, w_gate[...], preferred_element_type=F32)
    up_act = jnp.dot(x, w_up[...], preferred_element_type=F32)
    hidden[...] = (gate_act / (1.0 + jnp.exp(-gate_act)) * up_act).astype(BF16)
    tail = joined[:, features:].astype(F32)
    lane = lax.broadcasted_iota(jnp.int32, tail.shape, 1)
    here = (lane % experts == position) & (lane < PARTS * experts)
    row_gate = jnp.sum(jnp.where(here, tail, 0.0), axis=1, keepdims=True)
    h = hidden[...]
    step = 512
    for c in range(0, features, step):
        columns = slice(c, c + step)
        value = jnp.dot(h, w_down[:, columns], preferred_element_type=F32) * row_gate
        value = value.astype(BF16)
        kept[:, columns] = value[:half]
        sent[:, columns] = value[half:count]
        partner_kept[:, columns] = value[count : count + half]
        partner_sent[:, columns] = value[count + half :]


def expert_rows(order, mine, others, weights, experts):
    count, width = mine.shape
    features, hidden_units = weights[0].shape
    return order(
        functools.partial(expert_body, features, experts),
        "expert",
        [((n, features), BF16) for n in (count // 2,) * 4],
        (mine, others, *weights),
        scratch=[pltpu.VMEM((2 * count, width), BF16), pltpu.VMEM((2 * count, hidden_units), BF16)],
        vmem=6,
        flops=WEIGHT * 12 * count * features * hidden_units,
    )


def core_sum_body(sent, received, out):
    out[...] = (sent[...].astype(F32) + received[...].astype(F32)).astype(BF16)


def part_sum_body(kept, from_core, received, mine, passed):
    rows = mine.shape[0]

    def total(at):
        return (kept[at, :].astype(F32) + from_core[at, :].astype(F32)) + received[at, :].astype(F32)

    mine[...] = total(slice(0, rows))
    passed[...] = total(slice(rows, 2 * rows)).astype(BF16)


def plane_sum_body(mine, received, out):
    out[...] = (mine[...] + received[...].astype(F32)).astype(out.dtype)


def on_device_plane(
    tokens, routes, route_gates, placement, swap_flags, gate_weight, up_weight, down_weight
):
    rows, features = tokens.shape
    experts = placement.shape[0]
    weights = [gate_weight[0], up_weight[0], down_weight[0]]
    order = Order()
    own = labelled(order, tokens, routes, route_gates, placement, swap_flags)
    block, pair, mine, others = {0: own}, {}, {}, {}
    kept, sent, more_kept, more_sent, total = {}, {}, {}, {}, {}
    steps = range(1, NZ)
    from_z = {step: along_z(own, step) for step in steps}
    from_first = {0: over_first(own)}
    from_second = {}

    def inputs(kind, step):
        wide = features + TAIL
        if kind == "block":
            return block_body, [((rows, wide), BF16)], [from_z[step]]
        if kind == "pair":
            return pack_body, [((2 * rows, wide), BF16)], [block[step], from_first[step]]
        if kind == "mine":
            return pack_body, [((4 * rows, wide), BF16)], [pair[step], from_second[step]]
        if kind == "core":
            return core_sum_body, [((2 * rows, features), BF16)], [sent[step], more_sent[step]]
        if kind == "far":
            outs = [((rows, features), F32), ((rows, features), BF16)]
            return part_sum_body, outs, [kept[step], more_kept[step], sent[step]]
        if kind == "near":
            outs = [((rows, features), BF16 if step else F32)]
            return plane_sum_body, outs, [kept[step], sent[step]]
        outs = [((rows, features), BF16 if step == folds[-1] else F32)]
        return plane_sum_body, outs, [total[0], total[step]]

    def passed_on(kind, step, results):
        if kind == "block":
            [block[step]] = results
            from_first[step] = over_first(block[step])
        elif kind == "pair":
            [pair[step]] = results
            from_second[step] = over_second(pair[step])
        elif kind == "mine":
            [mine[step]] = results
            others[step] = over_core(mine[step])
        elif kind == "core":
            sent[step] = over_second(results[0])
        elif kind == "far":
            kept[step], sent[step] = results[0], over_first(results[1])
        elif kind == "near":
            total[step] = along_z(results[0], step) if step else results[0]
        else:
            [total[0]] = results

    folds = [int(name[-1]) for group in SEQUENCE for name in group.split() if name[:-1] == "fold"]
    for group in SEQUENCE:
        names = [(name[:-1], int(name[-1])) for name in group.split()]
        kind, step = names[0]
        if kind == "stage":
            weights[step] = staged(order, weights[step])
        elif kind == "expert":
            results = expert_rows(order, mine[step], others[step], weights, experts)
            kept[step], sent[step], more_kept[step], more_sent[step] = results
            more_sent[step] = over_core(more_sent[step])
            more_kept[step] = over_core(more_kept[step])
        else:
            results = together(order, [inputs(*name) for name in names], group is SEQUENCE[-1])
            for name, result in zip(names, results):
                passed_on(*name, result)
    return total[0]


def on_device_lanes(
    tokens, routes, route_gates, placement, swap_flags, gate_weight, up_weight, down_weight
):
    tok_dev, features = tokens.shape
    route_count = routes.shape[1]
    columns = lax.axis_size("expert")
    replicas = lax.axis_size("dp")
    slot_count = replicas // 2
    experts = slot_count * columns
    capacity = 2 * tok_dev * route_count // experts
    lane_count = experts * capacity
    expert_ids = jnp.arange(experts, dtype=jnp.int32)
    flat_routes = routes.reshape(-1)
    matches = (flat_routes[:, None] == expert_ids[None, :]).astype(jnp.int32)
    target = routed_position(flat_routes, holder_of(placement, swap_flags))
    ranking = jnp.sum(matches * (jnp.cumsum(matches, axis=0) - 1), axis=1)
    column = target // slot_count
    slot_id = target % slot_count
    lane_index = (slot_id * columns + column) * capacity + ranking
    pair_row = jnp.arange(tok_dev * route_count, dtype=jnp.int32) // route_count
    lane_hit = (jnp.arange(lane_count, dtype=jnp.int32)[:, None] == lane_index[None, :]).astype(F32)
    row_hit = (jnp.arange(tok_dev, dtype=jnp.int32)[:, None] == pair_row[None, :]).astype(F32)
    selector = jnp.dot(lane_hit, row_hit.T, precision=lax.Precision.HIGHEST).astype(BF16)
    combine = jnp.dot(
        row_hit * route_gates.reshape(-1)[None, :], lane_hit.T, precision=lax.Precision.HIGHEST
    )
    outgoing = jnp.dot(selector, tokens, preferred_element_type=F32).astype(BF16)
    outgoing = outgoing.reshape(slot_count, columns, capacity, features)

    def exchanged(value):
        value = lax.all_to_all(value, "dp", split_axis=0, concat_axis=0, tiled=True)
        return lax.all_to_all(value, "expert", split_axis=1, concat_axis=1, tiled=True)

    arrived = exchanged(jnp.repeat(outgoing, 2, axis=0))
    partial_value = expert_block(
        arrived.reshape(-1, features), gate_weight[0], up_weight[0], down_weight[0]
    ).astype(BF16)
    returned = exchanged(partial_value.reshape(replicas, columns, capacity, features))
    halves = returned.reshape(slot_count, 2, columns, capacity, features)
    summed = (halves[:, 0].astype(F32) + halves[:, 1].astype(F32)).astype(BF16)
    expert_rows = summed.reshape(lane_count, features)
    layer_out = jnp.dot(combine, expert_rows.astype(F32), precision=lax.Precision.HIGHEST)
    return layer_out.astype(BF16)


def solution(mesh):
    planes = mesh.shape["dp"] == NX * NC and mesh.shape["expert"] == NZ * NY
    return jax.shard_map(
        on_device_plane if planes else on_device_lanes,
        mesh=mesh,
        in_specs=(
            P(MESH_AXES, None),
            P(MESH_AXES, None),
            P(MESH_AXES, None),
            P(),
            P(),
            P("expert", None, "dp"),
            P("expert", None, "dp"),
            P("expert", "dp", None),
        ),
        out_specs=P(MESH_AXES, None),
        check_vma=False,
    )
```

```python
import functools

import jax
import jax.numpy as jnp
from jax import lax
from jax.experimental import pallas as pl
from jax.experimental.pallas import tpu as pltpu
from jax.sharding import PartitionSpec as P

MESH_AXES = ("dp", "expert")
F32 = jnp.float32
BF16 = jnp.bfloat16


def expert_block(received, w_gate, w_up, w_down):
    gate_act = jnp.dot(received, w_gate, preferred_element_type=F32)
    up_act = jnp.dot(received, w_up, preferred_element_type=F32)
    hidden = (jax.nn.silu(gate_act) * up_act).astype(BF16)
    return jnp.dot(hidden, w_down, preferred_element_type=F32)


def holder_of(placement, swap_flags):
    experts = placement.shape[0]
    ids = jnp.arange(experts, dtype=jnp.int32)
    flag_at = jnp.sum(jnp.where(placement[:, None] == ids[None, :], swap_flags[None, :], 0), axis=1)
    return jnp.where(flag_at == 0, placement, (placement + experts // 2) % experts)


def routed_position(routes, holder):
    ids = jnp.arange(holder.shape[0], dtype=jnp.int32)
    return jnp.sum(jnp.where(routes[..., None] == ids, holder, 0), axis=-1)


NX, NC, NZ, NY = 2, 2, 4, 2
TAIL = 128
PARTS = 3
PIECES = 4
SEQUENCE = (
    "stage1",
    "pair0",
    "block3",
    "block1",
    "stage0",
    "stage2",
    "block2 pair3 mine0 pair1",
    "pair2",
    "mine3",
    "expert0",
    "mine1",
    "expert3",
    "mine2 core3",
    "expert1",
    "expert2",
    "far3",
    "core0",
    "core2",
    "core1 near3",
    "far2",
    "far0",
    "far1",
    "near2",
    "near1 fold3",
    "fold2",
    "near0",
    "fold1",
)
WEIGHT = 20

IN_VMEM = pl.BlockSpec(memory_space=pltpu.VMEM)
IN_HBM = pl.BlockSpec(memory_space=pltpu.HBM)


def flat(x, c, z, y):
    return (x * NC + c) * (NZ * NY) + z * NY + y


def moved(value, to):
    pairs = [
        (flat(x, c, z, y), flat(*to(x, c, z, y)))
        for x in range(NX)
        for c in range(NC)
        for z in range(NZ)
        for y in range(NY)
    ]
    return lax.ppermute(value, MESH_AXES, pairs)


def over_first(value):
    return moved(value, lambda x, c, z, y: (x ^ 1 ^ c, c, z, y ^ c))


def over_second(value):
    return moved(value, lambda x, c, z, y: (x ^ c, c, z, y ^ 1 ^ c))


def over_core(value):
    return moved(value, lambda x, c, z, y: (x, 1 - c, z, y))


def along_z(value, by):
    return moved(value, lambda x, c, z, y: (x, c, z ^ by, y))


class Order:
    def __init__(self):
        self.mark = ()

    def __call__(self, body, name, outs, arrays, scratch=(), far=0, vmem=2, flops=0, last=False):
        near = [pltpu.with_memory_space_constraint(a, pltpu.VMEM) for a in (*arrays[far:], *self.mark)]
        placed = [pltpu.with_memory_space_constraint(a, pltpu.HBM) for a in arrays[:far]]
        given, skipped, made = len(arrays), len(self.mark), len(outs)
        marks = [] if last else [((8, 128), F32)]

        def marked(*refs):
            rest = refs[given + skipped :]
            for mark in rest[made : made + len(marks)]:
                mark[...] = jnp.zeros((8, 128), F32)
            body(*refs[:given], *rest[:made], *rest[made + len(marks) :])

        results = pl.pallas_call(
            marked,
            name=name,
            out_shape=[pltpu.VMEM(shape, dtype) for shape, dtype in (*outs, *marks)],
            in_specs=[IN_HBM] * far + [IN_VMEM] * len(near),
            out_specs=[IN_VMEM] * (made + len(marks)),
            scratch_shapes=list(scratch),
            compiler_params=pltpu.CompilerParams(vmem_limit_bytes=vmem * 2**20),
            cost_estimate=pl.CostEstimate(flops=flops, bytes_accessed=0, transcendentals=0),
        )(*placed, *near)
        self.mark = results[made:]
        return results[:made]


def rows_of(value):
    return value if isinstance(value, tuple) else (value, 0, value.shape[0])


def together(order, steps, last):
    arrays, reads, outs, writes, place = [], [], [], [], {}
    for run, _, shapes, values in steps:
        read = []
        for array, first, count in map(rows_of, values):
            known = [i for i, other in enumerate(arrays) if other is array]
            if not known:
                arrays.append(array)
            read.append((known[0] if known else len(arrays) - 1, first, count))
        reads.append(read)
        write = []
        for which, ((count, width), dtype) in enumerate(shapes):
            key = (run, which)
            if key not in place:
                place[key] = len(outs)
                outs.append([0, width, dtype])
            out = outs[place[key]]
            write.append((place[key], out[0], count))
            out[0] += count
        writes.append(write)

    def body(*refs):
        for (_, part, _, _), read, write in zip(steps, reads, writes):
            views = [refs[i].at[first : first + count] for i, first, count in read]
            views += [refs[len(arrays) + i].at[first : first + count] for i, first, count in write]
            part(*views)

    shapes = [((rows, width), dtype) for rows, width, dtype in outs]
    results = order(body, "sums", shapes, arrays, last=last)
    return results, writes


def label_body(
    tokens, routes, gates, placement, flags, out, token_at, route_at, gate_at, place_at, flag_at, sems
):
    rows, features = tokens.shape
    experts = placement.shape[0]
    pairs = (
        (placement, place_at),
        (flags, flag_at),
        (routes, route_at),
        (gates, gate_at),
        (tokens, token_at),
    )
    copies = [pltpu.make_async_copy(a, b, sems.at[i]) for i, (a, b) in enumerate(pairs)]
    for copy in copies:
        copy.start()
    for copy in copies:
        copy.wait()
    out[:, :features] = token_at[...]
    named = route_at[...].T
    row_gates = gate_at[...].T
    target = jnp.zeros_like(named)
    for x in range(experts):
        held = place_at[x]
        held = jnp.where(flag_at[held] == 0, held, (held + experts // 2) % experts)
        target = jnp.where(named == x, held, target)
    lane = lax.broadcasted_iota(jnp.int32, (rows, TAIL), 1)
    weight = jnp.zeros((rows, TAIL), F32)
    for k in range(named.shape[1]):
        weight += jnp.where(lane % experts == target[:, k : k + 1], row_gates[:, k : k + 1], 0.0)
    high = weight.astype(BF16)
    rest = weight - high.astype(F32)
    middle = rest.astype(BF16)
    low = (rest - middle.astype(F32)).astype(BF16)
    tail = jnp.where(lane < experts, high.astype(F32), 0.0)
    tail = jnp.where((lane >= experts) & (lane < 2 * experts), middle.astype(F32), tail)
    tail = jnp.where((lane >= 2 * experts) & (lane < PARTS * experts), low.astype(F32), tail)
    out[:, features:] = tail.astype(BF16)


def labelled(order, tokens, routes, route_gates, placement, swap_flags):
    rows, features = tokens.shape
    arrays = (tokens, routes.T, route_gates.T, placement, swap_flags)
    outs = [((rows, features + TAIL), BF16)]
    scratch = [pltpu.VMEM(a.shape, a.dtype) for a in arrays[:3]]
    scratch += [pltpu.SMEM(a.shape, a.dtype) for a in arrays[3:]]
    scratch.append(pltpu.SemaphoreType.DMA((len(arrays),)))
    [out] = order(label_body, "label", outs, arrays, scratch=scratch, far=len(arrays))
    return out


def stage_body(source, out, sems):
    size = source.shape[0] // PIECES
    pieces = [pl.ds(i * size, size) for i in range(PIECES)]
    copies = [
        pltpu.make_async_copy(source.at[piece], out.at[piece], sems.at[i])
        for i, piece in enumerate(pieces)
    ]
    for copy in copies:
        copy.start()
    for copy in copies:
        copy.wait()


def staged(order, weight):
    outs = [(weight.shape, weight.dtype)]
    scratch = [pltpu.SemaphoreType.DMA((PIECES,))]
    [result] = order(stage_body, "stage", outs, (weight,), scratch, far=1)
    return result


def pack_body(block, received, out):
    count = block.shape[0]
    out[:count, :] = block[...]
    out[count:, :] = received[...]


def block_body(received, out):
    out[...] = received[...]


def expert_body(features, experts, places, mine, others, w_gate, w_up, w_down, *refs):
    kept, sent, partner_kept, partner_sent, joined, hidden = refs
    count, half = places[0][1], kept.shape[0]
    mine, others = (ref.at[first : first + n] for ref, (first, n) in zip((mine, others), places))
    position = lax.axis_index("expert") * NX + lax.div(lax.axis_index("dp"), NC)
    joined[:count, :] = mine[...]
    joined[count:, :] = others[...]
    x = joined[:, :features]
    gate_act = jnp.dot(x, w_gate[...], preferred_element_type=F32)
    up_act = jnp.dot(x, w_up[...], preferred_element_type=F32)
    hidden[...] = (gate_act / (1.0 + jnp.exp(-gate_act)) * up_act).astype(BF16)
    tail = joined[:, features:].astype(F32)
    lane = lax.broadcasted_iota(jnp.int32, tail.shape, 1)
    here = (lane % experts == position) & (lane < PARTS * experts)
    row_gate = jnp.sum(jnp.where(here, tail, 0.0), axis=1, keepdims=True)
    h = hidden[...]
    step = 512
    for c in range(0, features, step):
        columns = slice(c, c + step)
        value = jnp.dot(h, w_down[:, columns], preferred_element_type=F32) * row_gate
        value = value.astype(BF16)
        kept[:, columns] = value[:half]
        sent[:, columns] = value[half:count]
        partner_kept[:, columns] = value[count : count + half]
        partner_sent[:, columns] = value[count + half :]


def expert_rows(order, mine, others, weights, experts):
    arrays, *places = zip(rows_of(mine), rows_of(others))
    places = tuple(zip(*places))
    count, width = places[0][1], arrays[0].shape[1]
    features, hidden_units = weights[0].shape
    return order(
        functools.partial(expert_body, features, experts, places),
        "expert",
        [((n, features), BF16) for n in (count // 2,) * 4],
        (*arrays, *weights),
        scratch=[pltpu.VMEM((2 * count, width), BF16), pltpu.VMEM((2 * count, hidden_units), BF16)],
        vmem=6,
        flops=WEIGHT * 12 * count * features * hidden_units,
    )


def core_sum_body(sent, received, out):
    out[...] = (sent[...].astype(F32) + received[...].astype(F32)).astype(BF16)


def part_sum_body(kept, from_core, received, mine, passed):
    rows = mine.shape[0]

    def total(at):
        return (kept[at, :].astype(F32) + from_core[at, :].astype(F32)) + received[at, :].astype(F32)

    mine[...] = total(slice(0, rows))
    passed[...] = total(slice(rows, 2 * rows)).astype(BF16)


def sum_body(*refs):
    *parts, out = refs
    total = parts[0][...].astype(F32)
    for part in parts[1:]:
        total += part[...].astype(F32)
    out[...] = total.astype(out.dtype)


def on_device_plane(
    tokens, routes, route_gates, placement, swap_flags, gate_weight, up_weight, down_weight
):
    rows, features = tokens.shape
    experts = placement.shape[0]
    weights = [gate_weight[0], up_weight[0], down_weight[0]]
    order = Order()
    own = labelled(order, tokens, routes, route_gates, placement, swap_flags)
    block, pair, mine, others = {0: own}, {}, {}, {}
    kept, sent, more_kept, more_sent, total = {}, {}, {}, {}, {}
    steps = range(1, NZ)
    from_z = {step: along_z(own, step) for step in steps}
    from_first = {0: over_first(own)}
    from_second = {}

    def inputs(kind, step):
        wide = features + TAIL
        if kind == "block":
            return block_body, [((rows, wide), BF16)], [from_z[step]]
        if kind == "pair":
            return pack_body, [((2 * rows, wide), BF16)], [block[step], from_first[step]]
        if kind == "mine":
            return pack_body, [((4 * rows, wide), BF16)], [pair[step], from_second[step]]
        if kind == "core":
            return core_sum_body, [((2 * rows, features), BF16)], [sent[step], more_sent[step]]
        if kind == "far":
            outs = [((rows, features), F32), ((rows, features), BF16)]
            return part_sum_body, outs, [kept[step], more_kept[step], sent[step]]
        if kind == "near" and step:
            return sum_body, [((rows, features), BF16)], [kept[step], sent[step]]
        parts = [total[step]] if kind == "fold" else [kept[step], sent[step]]
        outs = [((rows, features), BF16 if (kind, step) == final else F32)]
        return sum_body, outs, whole + parts

    def passed_on(kind, which, results, writes):
        made = [results[i] for i, _, _ in writes[0]]
        send = {"block": over_first, "pair": over_second, "mine": over_core, "core": over_second, "far": over_first}
        received = send[kind](made[-1]) if kind in send else None
        for step, write in zip(which, writes):
            (_, first, count) = write[-1]
            here, there = (made[-1], first, count), (received, first, count)
            if kind == "block":
                block[step], from_first[step] = here, there
            elif kind == "pair":
                pair[step], from_second[step] = here, there
            elif kind == "mine":
                mine[step], others[step] = here, there
            elif kind == "core":
                sent[step] = there
            elif kind == "far":
                kept[step], sent[step] = (made[0], *write[0][1:]), there
            elif kind == "near" and step:
                total[step] = along_z(made[0], step)
            else:
                whole[:] = made

    final = (SEQUENCE[-1][:-1], int(SEQUENCE[-1][-1]))
    whole = []
    for group in SEQUENCE:
        runs = [[(name[:-1], int(name[-1])) for name in run.split("+")] for run in group.split()]
        kind, step = runs[0][0]
        if kind == "stage":
            weights[step] = staged(order, weights[step])
        elif kind == "expert":
            results = expert_rows(order, mine[step], others[step], weights, experts)
            kept[step], sent[step], more_kept[step], more_sent[step] = results
            more_sent[step] = over_core(more_sent[step])
            more_kept[step] = over_core(more_kept[step])
        else:
            steps = [(i, *inputs(*name)) for i, run in enumerate(runs) for name in run]
            results, writes = together(order, steps, group is SEQUENCE[-1])
            for i, run in enumerate(runs):
                at = [write for step, write in zip(steps, writes) if step[0] == i]
                passed_on(run[0][0], [step for _, step in run], results, at)
    return whole[0]


def on_device_lanes(
    tokens, routes, route_gates, placement, swap_flags, gate_weight, up_weight, down_weight
):
    tok_dev, features = tokens.shape
    route_count = routes.shape[1]
    columns = lax.axis_size("expert")
    replicas = lax.axis_size("dp")
    slot_count = replicas // 2
    experts = slot_count * columns
    capacity = 2 * tok_dev * route_count // experts
    lane_count = experts * capacity
    expert_ids = jnp.arange(experts, dtype=jnp.int32)
    flat_routes = routes.reshape(-1)
    matches = (flat_routes[:, None] == expert_ids[None, :]).astype(jnp.int32)
    target = routed_position(flat_routes, holder_of(placement, swap_flags))
    ranking = jnp.sum(matches * (jnp.cumsum(matches, axis=0) - 1), axis=1)
    column = target // slot_count
    slot_id = target % slot_count
    lane_index = (slot_id * columns + column) * capacity + ranking
    pair_row = jnp.arange(tok_dev * route_count, dtype=jnp.int32) // route_count
    lane_hit = (jnp.arange(lane_count, dtype=jnp.int32)[:, None] == lane_index[None, :]).astype(F32)
    row_hit = (jnp.arange(tok_dev, dtype=jnp.int32)[:, None] == pair_row[None, :]).astype(F32)
    selector = jnp.dot(lane_hit, row_hit.T, precision=lax.Precision.HIGHEST).astype(BF16)
    combine = jnp.dot(
        row_hit * route_gates.reshape(-1)[None, :], lane_hit.T, precision=lax.Precision.HIGHEST
    )
    outgoing = jnp.dot(selector, tokens, preferred_element_type=F32).astype(BF16)
    outgoing = outgoing.reshape(slot_count, columns, capacity, features)

    def exchanged(value):
        value = lax.all_to_all(value, "dp", split_axis=0, concat_axis=0, tiled=True)
        return lax.all_to_all(value, "expert", split_axis=1, concat_axis=1, tiled=True)

    arrived = exchanged(jnp.repeat(outgoing, 2, axis=0))
    partial_value = expert_block(
        arrived.reshape(-1, features), gate_weight[0], up_weight[0], down_weight[0]
    ).astype(BF16)
    returned = exchanged(partial_value.reshape(replicas, columns, capacity, features))
    halves = returned.reshape(slot_count, 2, columns, capacity, features)
    summed = (halves[:, 0].astype(F32) + halves[:, 1].astype(F32)).astype(BF16)
    expert_rows = summed.reshape(lane_count, features)
    layer_out = jnp.dot(combine, expert_rows.astype(F32), precision=lax.Precision.HIGHEST)
    return layer_out.astype(BF16)


def solution(mesh):
    planes = mesh.shape["dp"] == NX * NC and mesh.shape["expert"] == NZ * NY
    return jax.shard_map(
        on_device_plane if planes else on_device_lanes,
        mesh=mesh,
        in_specs=(
            P(MESH_AXES, None),
            P(MESH_AXES, None),
            P(MESH_AXES, None),
            P(),
            P(),
            P("expert", None, "dp"),
            P("expert", None, "dp"),
            P("expert", "dp", None),
        ),
        out_specs=P(MESH_AXES, None),
        check_vma=False,
    )
```

```python
import functools

import jax
import jax.numpy as jnp
from jax import lax
from jax.experimental import pallas as pl
from jax.experimental.pallas import tpu as pltpu
from jax.sharding import PartitionSpec as P

MESH_AXES = ("dp", "expert")
F32 = jnp.float32
BF16 = jnp.bfloat16


def expert_block(received, w_gate, w_up, w_down):
    gate_act = jnp.dot(received, w_gate, preferred_element_type=F32)
    up_act = jnp.dot(received, w_up, preferred_element_type=F32)
    hidden = (jax.nn.silu(gate_act) * up_act).astype(BF16)
    return jnp.dot(hidden, w_down, preferred_element_type=F32)


def holder_of(placement, swap_flags):
    experts = placement.shape[0]
    ids = jnp.arange(experts, dtype=jnp.int32)
    flag_at = jnp.sum(jnp.where(placement[:, None] == ids[None, :], swap_flags[None, :], 0), axis=1)
    return jnp.where(flag_at == 0, placement, (placement + experts // 2) % experts)


def routed_position(routes, holder):
    ids = jnp.arange(holder.shape[0], dtype=jnp.int32)
    return jnp.sum(jnp.where(routes[..., None] == ids, holder, 0), axis=-1)


NX, NC, NZ, NY = 2, 2, 4, 2
TAIL = 128
PARTS = 3
PIECES = 4
SEQUENCE = (
    "stage1*",
    "pair0",
    "block3",
    "block1",
    "stage2",
    "stage0",
    "block2 pair3 mine0 pair1",
    "pair2",
    "mine3",
    "expert0",
    "expert3",
    "mine1",
    "mine2 core3*",
    "expert1",
    "expert2",
    "core0 far3*",
    "core2*",
    "core1 near3*",
    "far2*",
    "far1*",
    "near2",
    "near1 fold3*",
    "far0*",
    "fold2",
    "fold1*",
    "near0",
)
WEIGHT = 20
LONG = 10**10

IN_VMEM = pl.BlockSpec(memory_space=pltpu.VMEM)
IN_HBM = pl.BlockSpec(memory_space=pltpu.HBM)


def flat(x, c, z, y):
    return (x * NC + c) * (NZ * NY) + z * NY + y


def moved(value, to):
    pairs = [
        (flat(x, c, z, y), flat(*to(x, c, z, y)))
        for x in range(NX)
        for c in range(NC)
        for z in range(NZ)
        for y in range(NY)
    ]
    return lax.ppermute(value, MESH_AXES, pairs)


def over_first(value):
    return moved(value, lambda x, c, z, y: (x ^ 1 ^ c, c, z, y ^ c))


def over_second(value):
    return moved(value, lambda x, c, z, y: (x ^ c, c, z, y ^ 1 ^ c))


def over_core(value):
    return moved(value, lambda x, c, z, y: (x, 1 - c, z, y))


def along_z(value, by):
    return moved(value, lambda x, c, z, y: (x, c, z ^ by, y))


class Order:
    def __init__(self):
        self.mark = ()

    def __call__(self, body, name, outs, arrays, scratch=(), far=0, vmem=2, flops=0, last=False):
        near = [pltpu.with_memory_space_constraint(a, pltpu.VMEM) for a in (*arrays[far:], *self.mark)]
        placed = [pltpu.with_memory_space_constraint(a, pltpu.HBM) for a in arrays[:far]]
        given, skipped, made = len(arrays), len(self.mark), len(outs)
        marks = [] if last else [((8, 128), F32)]

        def marked(*refs):
            rest = refs[given + skipped :]
            for mark in rest[made : made + len(marks)]:
                mark[...] = jnp.zeros((8, 128), F32)
            body(*refs[:given], *rest[:made], *rest[made + len(marks) :])

        results = pl.pallas_call(
            marked,
            name=name,
            out_shape=[pltpu.VMEM(shape, dtype) for shape, dtype in (*outs, *marks)],
            in_specs=[IN_HBM] * far + [IN_VMEM] * len(near),
            out_specs=[IN_VMEM] * (made + len(marks)),
            scratch_shapes=list(scratch),
            compiler_params=pltpu.CompilerParams(vmem_limit_bytes=vmem * 2**20),
            cost_estimate=pl.CostEstimate(flops=flops, bytes_accessed=0, transcendentals=0),
        )(*placed, *near)
        self.mark = results[made:]
        return results[:made]


def rows_of(value):
    return value if isinstance(value, tuple) else (value, 0, value.shape[0])


def together(order, steps, last, flops):
    arrays, reads, outs, writes, place = [], [], [], [], {}
    for run, _, shapes, values in steps:
        read = []
        for array, first, count in map(rows_of, values):
            known = [i for i, other in enumerate(arrays) if other is array]
            if not known:
                arrays.append(array)
            read.append((known[0] if known else len(arrays) - 1, first, count))
        reads.append(read)
        write = []
        for which, ((count, width), dtype) in enumerate(shapes):
            key = (run, which)
            if key not in place:
                place[key] = len(outs)
                outs.append([0, width, dtype])
            out = outs[place[key]]
            write.append((place[key], out[0], count))
            out[0] += count
        writes.append(write)

    def body(*refs):
        for (_, part, _, _), read, write in zip(steps, reads, writes):
            views = [refs[i].at[first : first + count] for i, first, count in read]
            views += [refs[len(arrays) + i].at[first : first + count] for i, first, count in write]
            part(*views)

    shapes = [((rows, width), dtype) for rows, width, dtype in outs]
    results = order(body, "sums", shapes, arrays, flops=flops, last=last)
    return results, writes


def label_body(
    tokens, routes, gates, placement, flags, out, token_at, route_at, gate_at, place_at, flag_at, sems
):
    rows, features = tokens.shape
    experts = placement.shape[0]
    pairs = (
        (placement, place_at),
        (flags, flag_at),
        (routes, route_at),
        (gates, gate_at),
        (tokens, token_at),
    )
    copies = [pltpu.make_async_copy(a, b, sems.at[i]) for i, (a, b) in enumerate(pairs)]
    for copy in copies:
        copy.start()
    for copy in copies:
        copy.wait()
    out[:, :features] = token_at[...]
    named = route_at[...].T
    row_gates = gate_at[...].T
    target = jnp.zeros_like(named)
    for x in range(experts):
        held = place_at[x]
        held = jnp.where(flag_at[held] == 0, held, (held + experts // 2) % experts)
        target = jnp.where(named == x, held, target)
    lane = lax.broadcasted_iota(jnp.int32, (rows, TAIL), 1)
    weight = jnp.zeros((rows, TAIL), F32)
    for k in range(named.shape[1]):
        weight += jnp.where(lane % experts == target[:, k : k + 1], row_gates[:, k : k + 1], 0.0)
    high = weight.astype(BF16)
    rest = weight - high.astype(F32)
    middle = rest.astype(BF16)
    low = (rest - middle.astype(F32)).astype(BF16)
    tail = jnp.where(lane < experts, high.astype(F32), 0.0)
    tail = jnp.where((lane >= experts) & (lane < 2 * experts), middle.astype(F32), tail)
    tail = jnp.where((lane >= 2 * experts) & (lane < PARTS * experts), low.astype(F32), tail)
    out[:, features:] = tail.astype(BF16)


def labelled(order, tokens, routes, route_gates, placement, swap_flags):
    rows, features = tokens.shape
    arrays = (tokens, routes.T, route_gates.T, placement, swap_flags)
    outs = [((rows, features + TAIL), BF16)]
    scratch = [pltpu.VMEM(a.shape, a.dtype) for a in arrays[:3]]
    scratch += [pltpu.SMEM(a.shape, a.dtype) for a in arrays[3:]]
    scratch.append(pltpu.SemaphoreType.DMA((len(arrays),)))
    [out] = order(label_body, "label", outs, arrays, scratch=scratch, far=len(arrays))
    return out


def stage_body(*refs):
    *pairs, sems = refs
    count = len(pairs) // 2
    copies = []
    for i, (source, out) in enumerate(zip(pairs[:count], pairs[count:])):
        size = source.shape[0] // PIECES
        for j in range(PIECES):
            piece = pl.ds(j * size, size)
            copies.append(pltpu.make_async_copy(source.at[piece], out.at[piece], sems.at[i, j]))
    for copy in copies:
        copy.start()
    for copy in copies:
        copy.wait()


def staged(order, weights, flops):
    outs = [(w.shape, w.dtype) for w in weights]
    scratch = [pltpu.SemaphoreType.DMA((len(weights), PIECES))]
    return order(stage_body, "stage", outs, weights, scratch, far=len(weights), flops=flops)


def pack_body(block, received, out):
    count = block.shape[0]
    out[:count, :] = block[...]
    out[count:, :] = received[...]


def block_body(received, out):
    out[...] = received[...]


def expert_body(features, experts, places, mine, others, w_gate, w_up, w_down, *refs):
    kept, sent, partner_kept, partner_sent, joined, hidden = refs
    count, half = places[0][1], kept.shape[0]
    mine, others = (ref.at[first : first + n] for ref, (first, n) in zip((mine, others), places))
    position = lax.axis_index("expert") * NX + lax.div(lax.axis_index("dp"), NC)
    joined[:count, :] = mine[...]
    joined[count:, :] = others[...]
    x = joined[:, :features]
    gate_act = jnp.dot(x, w_gate[...], preferred_element_type=F32)
    up_act = jnp.dot(x, w_up[...], preferred_element_type=F32)
    hidden[...] = (gate_act / (1.0 + jnp.exp(-gate_act)) * up_act).astype(BF16)
    tail = joined[:, features:].astype(F32)
    lane = lax.broadcasted_iota(jnp.int32, tail.shape, 1)
    here = (lane % experts == position) & (lane < PARTS * experts)
    row_gate = jnp.sum(jnp.where(here, tail, 0.0), axis=1, keepdims=True)
    h = hidden[...]
    step = 512
    for c in range(0, features, step):
        columns = slice(c, c + step)
        value = jnp.dot(h, w_down[:, columns], preferred_element_type=F32) * row_gate
        value = value.astype(BF16)
        kept[:, columns] = value[:half]
        sent[:, columns] = value[half:count]
        partner_kept[:, columns] = value[count : count + half]
        partner_sent[:, columns] = value[count + half :]


def expert_rows(order, mine, others, weights, experts):
    arrays, *places = zip(rows_of(mine), rows_of(others))
    places = tuple(zip(*places))
    count, width = places[0][1], arrays[0].shape[1]
    features, hidden_units = weights[0].shape
    return order(
        functools.partial(expert_body, features, experts, places),
        "expert",
        [((n, features), BF16) for n in (count // 2,) * 4],
        (*arrays, *weights),
        scratch=[pltpu.VMEM((2 * count, width), BF16), pltpu.VMEM((2 * count, hidden_units), BF16)],
        vmem=6,
        flops=WEIGHT * 12 * count * features * hidden_units,
    )


def core_sum_body(sent, received, out):
    out[...] = (sent[...].astype(F32) + received[...].astype(F32)).astype(BF16)


def part_sum_body(kept, from_core, received, mine, passed):
    rows = mine.shape[0]

    def total(at):
        return (kept[at, :].astype(F32) + from_core[at, :].astype(F32)) + received[at, :].astype(F32)

    mine[...] = total(slice(0, rows))
    passed[...] = total(slice(rows, 2 * rows)).astype(BF16)


def sum_body(*refs):
    *parts, out = refs
    total = parts[0][...].astype(F32)
    for part in parts[1:]:
        total += part[...].astype(F32)
    out[...] = total.astype(out.dtype)


def on_device_plane(
    tokens, routes, route_gates, placement, swap_flags, gate_weight, up_weight, down_weight
):
    rows, features = tokens.shape
    experts = placement.shape[0]
    weights = [gate_weight[0], up_weight[0], down_weight[0]]
    order = Order()
    own = labelled(order, tokens, routes, route_gates, placement, swap_flags)
    block, pair, mine, others = {0: own}, {}, {}, {}
    kept, sent, more_kept, more_sent, total = {}, {}, {}, {}, {}
    steps = range(1, NZ)
    from_z = {step: along_z(own, step) for step in steps}
    from_first = {0: over_first(own)}
    from_second = {}

    def inputs(kind, step):
        wide = features + TAIL
        if kind == "block":
            return block_body, [((rows, wide), BF16)], [from_z[step]]
        if kind == "pair":
            return pack_body, [((2 * rows, wide), BF16)], [block[step], from_first[step]]
        if kind == "mine":
            return pack_body, [((4 * rows, wide), BF16)], [pair[step], from_second[step]]
        if kind == "core":
            return core_sum_body, [((2 * rows, features), BF16)], [sent[step], more_sent[step]]
        if kind == "far":
            outs = [((rows, features), F32), ((rows, features), BF16)]
            return part_sum_body, outs, [kept[step], more_kept[step], sent[step]]
        if kind == "near" and step:
            return sum_body, [((rows, features), BF16)], [kept[step], sent[step]]
        parts = [total[step]] if kind == "fold" else [kept[step], sent[step]]
        outs = [((rows, features), BF16 if (kind, step) == final else F32)]
        return sum_body, outs, whole + parts

    def passed_on(kind, which, results, writes):
        made = [results[i] for i, _, _ in writes[0]]
        send = {"block": over_first, "pair": over_second, "mine": over_core, "core": over_second, "far": over_first}
        received = send[kind](made[-1]) if kind in send else None
        for step, write in zip(which, writes):
            (_, first, count) = write[-1]
            here, there = (made[-1], first, count), (received, first, count)
            if kind == "block":
                block[step], from_first[step] = here, there
            elif kind == "pair":
                pair[step], from_second[step] = here, there
            elif kind == "mine":
                mine[step], others[step] = here, there
            elif kind == "core":
                sent[step] = there
            elif kind == "far":
                kept[step], sent[step] = (made[0], *write[0][1:]), there
            elif kind == "near" and step:
                total[step] = along_z(made[0], step)
            else:
                whole[:] = made

    final = (SEQUENCE[-1][:-1], int(SEQUENCE[-1][-1]))
    whole = []
    for group in SEQUENCE:
        group, flops = group.rstrip("*"), LONG if group.endswith("*") else 0
        runs = [[(name[:-1], int(name[-1])) for name in run.split("+")] for run in group.split()]
        kind, step = runs[0][0]
        if kind == "stage":
            which = [step for _, step in runs[0]]
            for step, weight in zip(which, staged(order, [weights[i] for i in which], flops)):
                weights[step] = weight
        elif kind == "expert":
            results = expert_rows(order, mine[step], others[step], weights, experts)
            kept[step], sent[step], more_kept[step], more_sent[step] = results
            more_sent[step] = over_core(more_sent[step])
            more_kept[step] = over_core(more_kept[step])
        else:
            steps = [(i, *inputs(*name)) for i, run in enumerate(runs) for name in run]
            results, writes = together(order, steps, group == SEQUENCE[-1], flops)
            for i, run in enumerate(runs):
                at = [write for step, write in zip(steps, writes) if step[0] == i]
                passed_on(run[0][0], [step for _, step in run], results, at)
    return whole[0]


def on_device_lanes(
    tokens, routes, route_gates, placement, swap_flags, gate_weight, up_weight, down_weight
):
    tok_dev, features = tokens.shape
    route_count = routes.shape[1]
    columns = lax.axis_size("expert")
    replicas = lax.axis_size("dp")
    slot_count = replicas // 2
    experts = slot_count * columns
    capacity = 2 * tok_dev * route_count // experts
    lane_count = experts * capacity
    expert_ids = jnp.arange(experts, dtype=jnp.int32)
    flat_routes = routes.reshape(-1)
    matches = (flat_routes[:, None] == expert_ids[None, :]).astype(jnp.int32)
    target = routed_position(flat_routes, holder_of(placement, swap_flags))
    ranking = jnp.sum(matches * (jnp.cumsum(matches, axis=0) - 1), axis=1)
    column = target // slot_count
    slot_id = target % slot_count
    lane_index = (slot_id * columns + column) * capacity + ranking
    pair_row = jnp.arange(tok_dev * route_count, dtype=jnp.int32) // route_count
    lane_hit = (jnp.arange(lane_count, dtype=jnp.int32)[:, None] == lane_index[None, :]).astype(F32)
    row_hit = (jnp.arange(tok_dev, dtype=jnp.int32)[:, None] == pair_row[None, :]).astype(F32)
    selector = jnp.dot(lane_hit, row_hit.T, precision=lax.Precision.HIGHEST).astype(BF16)
    combine = jnp.dot(
        row_hit * route_gates.reshape(-1)[None, :], lane_hit.T, precision=lax.Precision.HIGHEST
    )
    outgoing = jnp.dot(selector, tokens, preferred_element_type=F32).astype(BF16)
    outgoing = outgoing.reshape(slot_count, columns, capacity, features)

    def exchanged(value):
        value = lax.all_to_all(value, "dp", split_axis=0, concat_axis=0, tiled=True)
        return lax.all_to_all(value, "expert", split_axis=1, concat_axis=1, tiled=True)

    arrived = exchanged(jnp.repeat(outgoing, 2, axis=0))
    partial_value = expert_block(
        arrived.reshape(-1, features), gate_weight[0], up_weight[0], down_weight[0]
    ).astype(BF16)
    returned = exchanged(partial_value.reshape(replicas, columns, capacity, features))
    halves = returned.reshape(slot_count, 2, columns, capacity, features)
    summed = (halves[:, 0].astype(F32) + halves[:, 1].astype(F32)).astype(BF16)
    expert_rows = summed.reshape(lane_count, features)
    layer_out = jnp.dot(combine, expert_rows.astype(F32), precision=lax.Precision.HIGHEST)
    return layer_out.astype(BF16)


def solution(mesh):
    planes = mesh.shape["dp"] == NX * NC and mesh.shape["expert"] == NZ * NY
    return jax.shard_map(
        on_device_plane if planes else on_device_lanes,
        mesh=mesh,
        in_specs=(
            P(MESH_AXES, None),
            P(MESH_AXES, None),
            P(MESH_AXES, None),
            P(),
            P(),
            P("expert", None, "dp"),
            P("expert", None, "dp"),
            P("expert", "dp", None),
        ),
        out_specs=P(MESH_AXES, None),
        check_vma=False,
    )
```

```python
import functools

import jax
import jax.numpy as jnp
from jax import lax
from jax.experimental import pallas as pl
from jax.experimental.pallas import tpu as pltpu
from jax.sharding import PartitionSpec as P

MESH_AXES = ("dp", "expert")
F32 = jnp.float32
BF16 = jnp.bfloat16


def expert_block(received, w_gate, w_up, w_down):
    gate_act = jnp.dot(received, w_gate, preferred_element_type=F32)
    up_act = jnp.dot(received, w_up, preferred_element_type=F32)
    hidden = (jax.nn.silu(gate_act) * up_act).astype(BF16)
    return jnp.dot(hidden, w_down, preferred_element_type=F32)


def holder_of(placement, swap_flags):
    experts = placement.shape[0]
    ids = jnp.arange(experts, dtype=jnp.int32)
    flag_at = jnp.sum(jnp.where(placement[:, None] == ids[None, :], swap_flags[None, :], 0), axis=1)
    return jnp.where(flag_at == 0, placement, (placement + experts // 2) % experts)


def routed_position(routes, holder):
    ids = jnp.arange(holder.shape[0], dtype=jnp.int32)
    return jnp.sum(jnp.where(routes[..., None] == ids, holder, 0), axis=-1)


NX, NC, NZ, NY = 2, 2, 4, 2
TAIL = 128
PARTS = 3
PIECES = 4
SEQUENCE = (
    "stage1*",
    "pair0",
    "block3",
    "block1",
    "stage2",
    "stage0",
    "block2 pair3 mine0 pair1",
    "pair2",
    "mine3",
    "expert0",
    "expert3",
    "mine1",
    "mine2 core3*",
    "expert1",
    "expert2",
    "far3*",
    "core2*",
    "core0*",
    "core1 near3*",
    "far2*",
    "far1*",
    "near2",
    "near1 fold3*",
    "far0*",
    "fold2",
    "fold1*",
    "near0",
)
WEIGHT = 20
LONG = 10**10

IN_VMEM = pl.BlockSpec(memory_space=pltpu.VMEM)
IN_HBM = pl.BlockSpec(memory_space=pltpu.HBM)


def flat(x, c, z, y):
    return (x * NC + c) * (NZ * NY) + z * NY + y


def moved(value, to):
    pairs = [
        (flat(x, c, z, y), flat(*to(x, c, z, y)))
        for x in range(NX)
        for c in range(NC)
        for z in range(NZ)
        for y in range(NY)
    ]
    return lax.ppermute(value, MESH_AXES, pairs)


def over_first(value):
    return moved(value, lambda x, c, z, y: (x ^ 1 ^ c, c, z, y ^ c))


def over_second(value):
    return moved(value, lambda x, c, z, y: (x ^ c, c, z, y ^ 1 ^ c))


def over_core(value):
    return moved(value, lambda x, c, z, y: (x, 1 - c, z, y))


def along_z(value, by):
    return moved(value, lambda x, c, z, y: (x, c, z ^ by, y))


class Order:
    def __init__(self):
        self.mark = ()

    def __call__(self, body, name, outs, arrays, scratch=(), far=0, vmem=2, flops=0, last=False):
        near = [pltpu.with_memory_space_constraint(a, pltpu.VMEM) for a in (*arrays[far:], *self.mark)]
        placed = [pltpu.with_memory_space_constraint(a, pltpu.HBM) for a in arrays[:far]]
        given, skipped, made = len(arrays), len(self.mark), len(outs)
        marks = [] if last else [((8, 128), F32)]

        def marked(*refs):
            rest = refs[given + skipped :]
            for mark in rest[made : made + len(marks)]:
                mark[...] = jnp.zeros((8, 128), F32)
            body(*refs[:given], *rest[:made], *rest[made + len(marks) :])

        results = pl.pallas_call(
            marked,
            name=name,
            out_shape=[pltpu.VMEM(shape, dtype) for shape, dtype in (*outs, *marks)],
            in_specs=[IN_HBM] * far + [IN_VMEM] * len(near),
            out_specs=[IN_VMEM] * (made + len(marks)),
            scratch_shapes=list(scratch),
            compiler_params=pltpu.CompilerParams(vmem_limit_bytes=vmem * 2**20),
            cost_estimate=pl.CostEstimate(flops=flops, bytes_accessed=0, transcendentals=0),
        )(*placed, *near)
        self.mark = results[made:]
        return results[:made]


def rows_of(value):
    return value if isinstance(value, tuple) else (value, 0, value.shape[0])


def together(order, steps, last, flops):
    arrays, reads, outs, writes, place = [], [], [], [], {}
    for run, _, shapes, values in steps:
        read = []
        for array, first, count in map(rows_of, values):
            known = [i for i, other in enumerate(arrays) if other is array]
            if not known:
                arrays.append(array)
            read.append((known[0] if known else len(arrays) - 1, first, count))
        reads.append(read)
        write = []
        for which, ((count, width), dtype) in enumerate(shapes):
            key = (run, which)
            if key not in place:
                place[key] = len(outs)
                outs.append([0, width, dtype])
            out = outs[place[key]]
            write.append((place[key], out[0], count))
            out[0] += count
        writes.append(write)

    def body(*refs):
        for (_, part, _, _), read, write in zip(steps, reads, writes):
            views = [refs[i].at[first : first + count] for i, first, count in read]
            views += [refs[len(arrays) + i].at[first : first + count] for i, first, count in write]
            part(*views)

    shapes = [((rows, width), dtype) for rows, width, dtype in outs]
    results = order(body, "sums", shapes, arrays, flops=flops, last=last)
    return results, writes


def label_body(
    tokens, routes, gates, placement, flags, out, token_at, route_at, gate_at, place_at, flag_at, sems
):
    rows, features = tokens.shape
    experts = placement.shape[0]
    pairs = (
        (placement, place_at),
        (flags, flag_at),
        (routes, route_at),
        (gates, gate_at),
        (tokens, token_at),
    )
    copies = [pltpu.make_async_copy(a, b, sems.at[i]) for i, (a, b) in enumerate(pairs)]
    for copy in copies:
        copy.start()
    for copy in copies:
        copy.wait()
    out[:, :features] = token_at[...]
    named = route_at[...].T
    row_gates = gate_at[...].T
    target = jnp.zeros_like(named)
    for x in range(experts):
        held = place_at[x]
        held = jnp.where(flag_at[held] == 0, held, (held + experts // 2) % experts)
        target = jnp.where(named == x, held, target)
    lane = lax.broadcasted_iota(jnp.int32, (rows, TAIL), 1)
    weight = jnp.zeros((rows, TAIL), F32)
    for k in range(named.shape[1]):
        weight += jnp.where(lane % experts == target[:, k : k + 1], row_gates[:, k : k + 1], 0.0)
    high = weight.astype(BF16)
    rest = weight - high.astype(F32)
    middle = rest.astype(BF16)
    low = (rest - middle.astype(F32)).astype(BF16)
    tail = jnp.where(lane < experts, high.astype(F32), 0.0)
    tail = jnp.where((lane >= experts) & (lane < 2 * experts), middle.astype(F32), tail)
    tail = jnp.where((lane >= 2 * experts) & (lane < PARTS * experts), low.astype(F32), tail)
    out[:, features:] = tail.astype(BF16)


def labelled(order, tokens, routes, route_gates, placement, swap_flags):
    rows, features = tokens.shape
    arrays = (tokens, routes.T, route_gates.T, placement, swap_flags)
    outs = [((rows, features + TAIL), BF16)]
    scratch = [pltpu.VMEM(a.shape, a.dtype) for a in arrays[:3]]
    scratch += [pltpu.SMEM(a.shape, a.dtype) for a in arrays[3:]]
    scratch.append(pltpu.SemaphoreType.DMA((len(arrays),)))
    [out] = order(label_body, "label", outs, arrays, scratch=scratch, far=len(arrays))
    return out


def stage_body(*refs):
    *pairs, sems = refs
    count = len(pairs) // 2
    copies = []
    for i, (source, out) in enumerate(zip(pairs[:count], pairs[count:])):
        size = source.shape[0] // PIECES
        for j in range(PIECES):
            piece = pl.ds(j * size, size)
            copies.append(pltpu.make_async_copy(source.at[piece], out.at[piece], sems.at[i, j]))
    for copy in copies:
        copy.start()
    for copy in copies:
        copy.wait()


def staged(order, weights, flops):
    outs = [(w.shape, w.dtype) for w in weights]
    scratch = [pltpu.SemaphoreType.DMA((len(weights), PIECES))]
    return order(stage_body, "stage", outs, weights, scratch, far=len(weights), flops=flops)


def pack_body(block, received, out):
    count = block.shape[0]
    out[:count, :] = block[...]
    out[count:, :] = received[...]


def block_body(received, out):
    out[...] = received[...]


def expert_body(features, experts, places, mine, others, w_gate, w_up, w_down, *refs):
    kept, sent, partner_kept, partner_sent, joined, hidden = refs
    count, half = places[0][1], kept.shape[0]
    mine, others = (ref.at[first : first + n] for ref, (first, n) in zip((mine, others), places))
    position = lax.axis_index("expert") * NX + lax.div(lax.axis_index("dp"), NC)
    joined[:count, :] = mine[...]
    joined[count:, :] = others[...]
    x = joined[:, :features]
    gate_act = jnp.dot(x, w_gate[...], preferred_element_type=F32)
    up_act = jnp.dot(x, w_up[...], preferred_element_type=F32)
    hidden[...] = (gate_act / (1.0 + jnp.exp(-gate_act)) * up_act).astype(BF16)
    tail = joined[:, features:].astype(F32)
    lane = lax.broadcasted_iota(jnp.int32, tail.shape, 1)
    here = (lane % experts == position) & (lane < PARTS * experts)
    row_gate = jnp.sum(jnp.where(here, tail, 0.0), axis=1, keepdims=True)
    h = hidden[...]
    step = 512
    for c in range(0, features, step):
        columns = slice(c, c + step)
        value = jnp.dot(h, w_down[:, columns], preferred_element_type=F32) * row_gate
        value = value.astype(BF16)
        kept[:, columns] = value[:half]
        sent[:, columns] = value[half:count]
        partner_kept[:, columns] = value[count : count + half]
        partner_sent[:, columns] = value[count + half :]


def expert_rows(order, mine, others, weights, experts):
    arrays, *places = zip(rows_of(mine), rows_of(others))
    places = tuple(zip(*places))
    count, width = places[0][1], arrays[0].shape[1]
    features, hidden_units = weights[0].shape
    return order(
        functools.partial(expert_body, features, experts, places),
        "expert",
        [((n, features), BF16) for n in (count // 2,) * 4],
        (*arrays, *weights),
        scratch=[pltpu.VMEM((2 * count, width), BF16), pltpu.VMEM((2 * count, hidden_units), BF16)],
        vmem=6,
        flops=WEIGHT * 12 * count * features * hidden_units,
    )


def core_sum_body(sent, received, out):
    out[...] = (sent[...].astype(F32) + received[...].astype(F32)).astype(BF16)


def part_sum_body(kept, from_core, received, mine, passed):
    rows = mine.shape[0]

    def total(at):
        return (kept[at, :].astype(F32) + from_core[at, :].astype(F32)) + received[at, :].astype(F32)

    mine[...] = total(slice(0, rows))
    passed[...] = total(slice(rows, 2 * rows)).astype(BF16)


def sum_body(*refs):
    *parts, out = refs
    total = parts[0][...].astype(F32)
    for part in parts[1:]:
        total += part[...].astype(F32)
    out[...] = total.astype(out.dtype)


def on_device_plane(
    tokens, routes, route_gates, placement, swap_flags, gate_weight, up_weight, down_weight
):
    rows, features = tokens.shape
    experts = placement.shape[0]
    weights = [gate_weight[0], up_weight[0], down_weight[0]]
    order = Order()
    own = labelled(order, tokens, routes, route_gates, placement, swap_flags)
    block, pair, mine, others = {0: own}, {}, {}, {}
    kept, sent, more_kept, more_sent, total = {}, {}, {}, {}, {}
    steps = range(1, NZ)
    from_z = {step: along_z(own, step) for step in steps}
    from_first = {0: over_first(own)}
    from_second = {}

    def inputs(kind, step):
        wide = features + TAIL
        if kind == "block":
            return block_body, [((rows, wide), BF16)], [from_z[step]]
        if kind == "pair":
            return pack_body, [((2 * rows, wide), BF16)], [block[step], from_first[step]]
        if kind == "mine":
            return pack_body, [((4 * rows, wide), BF16)], [pair[step], from_second[step]]
        if kind == "core":
            return core_sum_body, [((2 * rows, features), BF16)], [sent[step], more_sent[step]]
        if kind == "far":
            outs = [((rows, features), F32), ((rows, features), BF16)]
            return part_sum_body, outs, [kept[step], more_kept[step], sent[step]]
        if kind == "near" and step:
            return sum_body, [((rows, features), BF16)], [kept[step], sent[step]]
        parts = [total[step]] if kind == "fold" else [kept[step], sent[step]]
        outs = [((rows, features), BF16 if (kind, step) == final else F32)]
        return sum_body, outs, whole + parts

    def passed_on(kind, which, results, writes):
        made = [results[i] for i, _, _ in writes[0]]
        send = {"block": over_first, "pair": over_second, "mine": over_core, "core": over_second, "far": over_first}
        received = send[kind](made[-1]) if kind in send else None
        for step, write in zip(which, writes):
            (_, first, count) = write[-1]
            here, there = (made[-1], first, count), (received, first, count)
            if kind == "block":
                block[step], from_first[step] = here, there
            elif kind == "pair":
                pair[step], from_second[step] = here, there
            elif kind == "mine":
                mine[step], others[step] = here, there
            elif kind == "core":
                sent[step] = there
            elif kind == "far":
                kept[step], sent[step] = (made[0], *write[0][1:]), there
            elif kind == "near" and step:
                total[step] = along_z(made[0], step)
            else:
                whole[:] = made

    final = (SEQUENCE[-1][:-1], int(SEQUENCE[-1][-1]))
    whole = []
    for group in SEQUENCE:
        group, flops = group.rstrip("*"), LONG if group.endswith("*") else 0
        runs = [[(name[:-1], int(name[-1])) for name in run.split("+")] for run in group.split()]
        kind, step = runs[0][0]
        if kind == "stage":
            which = [step for _, step in runs[0]]
            for step, weight in zip(which, staged(order, [weights[i] for i in which], flops)):
                weights[step] = weight
        elif kind == "expert":
            results = expert_rows(order, mine[step], others[step], weights, experts)
            kept[step], sent[step], more_kept[step], more_sent[step] = results
            more_sent[step] = over_core(more_sent[step])
            more_kept[step] = over_core(more_kept[step])
        else:
            steps = [(i, *inputs(*name)) for i, run in enumerate(runs) for name in run]
            results, writes = together(order, steps, group == SEQUENCE[-1], flops)
            for i, run in enumerate(runs):
                at = [write for step, write in zip(steps, writes) if step[0] == i]
                passed_on(run[0][0], [step for _, step in run], results, at)
    return whole[0]


def on_device_lanes(
    tokens, routes, route_gates, placement, swap_flags, gate_weight, up_weight, down_weight
):
    tok_dev, features = tokens.shape
    route_count = routes.shape[1]
    columns = lax.axis_size("expert")
    replicas = lax.axis_size("dp")
    slot_count = replicas // 2
    experts = slot_count * columns
    capacity = 2 * tok_dev * route_count // experts
    lane_count = experts * capacity
    expert_ids = jnp.arange(experts, dtype=jnp.int32)
    flat_routes = routes.reshape(-1)
    matches = (flat_routes[:, None] == expert_ids[None, :]).astype(jnp.int32)
    target = routed_position(flat_routes, holder_of(placement, swap_flags))
    ranking = jnp.sum(matches * (jnp.cumsum(matches, axis=0) - 1), axis=1)
    column = target // slot_count
    slot_id = target % slot_count
    lane_index = (slot_id * columns + column) * capacity + ranking
    pair_row = jnp.arange(tok_dev * route_count, dtype=jnp.int32) // route_count
    lane_hit = (jnp.arange(lane_count, dtype=jnp.int32)[:, None] == lane_index[None, :]).astype(F32)
    row_hit = (jnp.arange(tok_dev, dtype=jnp.int32)[:, None] == pair_row[None, :]).astype(F32)
    selector = jnp.dot(lane_hit, row_hit.T, precision=lax.Precision.HIGHEST).astype(BF16)
    combine = jnp.dot(
        row_hit * route_gates.reshape(-1)[None, :], lane_hit.T, precision=lax.Precision.HIGHEST
    )
    outgoing = jnp.dot(selector, tokens, preferred_element_type=F32).astype(BF16)
    outgoing = outgoing.reshape(slot_count, columns, capacity, features)

    def exchanged(value):
        value = lax.all_to_all(value, "dp", split_axis=0, concat_axis=0, tiled=True)
        return lax.all_to_all(value, "expert", split_axis=1, concat_axis=1, tiled=True)

    arrived = exchanged(jnp.repeat(outgoing, 2, axis=0))
    partial_value = expert_block(
        arrived.reshape(-1, features), gate_weight[0], up_weight[0], down_weight[0]
    ).astype(BF16)
    returned = exchanged(partial_value.reshape(replicas, columns, capacity, features))
    halves = returned.reshape(slot_count, 2, columns, capacity, features)
    summed = (halves[:, 0].astype(F32) + halves[:, 1].astype(F32)).astype(BF16)
    expert_rows = summed.reshape(lane_count, features)
    layer_out = jnp.dot(combine, expert_rows.astype(F32), precision=lax.Precision.HIGHEST)
    return layer_out.astype(BF16)


def solution(mesh):
    planes = mesh.shape["dp"] == NX * NC and mesh.shape["expert"] == NZ * NY
    return jax.shard_map(
        on_device_plane if planes else on_device_lanes,
        mesh=mesh,
        in_specs=(
            P(MESH_AXES, None),
            P(MESH_AXES, None),
            P(MESH_AXES, None),
            P(),
            P(),
            P("expert", None, "dp"),
            P("expert", None, "dp"),
            P("expert", "dp", None),
        ),
        out_specs=P(MESH_AXES, None),
        check_vma=False,
    )
```
